128 devices in a mesh: ax: 8 (over y, z_lo), ay: 16 (over z_hi, x, core).
Axes of the slice: x: 4, y: 4, z: 4 (z_hi: 2, z_lo: 2; z = z_hi * 2 + z_lo), core: 2. Of those that a mesh axis runs over, the one named last changes fastest.
Arguments:
- noise: float32 [16, 2048, 4096], P(None, ('ax', 'ay')), may hold values from -6 to 6
- kappa: float32 [16, 2048, 4096], P(None, 'ax', 'ay'), may hold values from 0.05 to 2
- mask: int32 [2048, 4096], P('ax', 'ay'), may hold values 0 or 1
Outputs:
- sample: float32 [16, 2048, 4096], P(None, 'ax', 'ay')
The draws below stay inside these ranges and needn't reach their ends.
All inputs are finite; a program needn't handle non-finite values. No bound on the sum of `mask` on one device may be relied on, other than what follows from the above.
Results may differ from the reference program's by a relative error of at most 0.00002.
Values sent between devices are 32-bit elements; how exact they have to be, the bound alone decides.
A program may use at most 128 MiB of HBM per device.

```python
import math
import jax
import jax.numpy as jnp

NZ = 16
NX = 2048
NY = 4096


def touch_ends(values, stream_key, low, top_value):
    extent = values.shape
    index_at = [jax.random.randint(jax.random.fold_in(stream_key, axis), (), 0, extent[axis]) for axis in range(len(extent))]
    values = values.at[tuple(index_at)].set(low)
    longest = extent.index(max(extent))
    index_at[longest] = (index_at[longest] + 1) % extent[longest]
    return values.at[tuple(index_at)].set(top_value)


def block_scale(key, dims, split, smallest, high):
    def one(dim, shards_of):
        draws = jax.random.uniform(jax.random.fold_in(jax.random.fold_in(key, 6), dim), (shards_of,), jnp.float32, smallest / len(split), high / len(split))
        return jnp.repeat(jnp.exp(draws), dims[dim] // shards_of).reshape((-1,) + (1,) * (len(dims) - dim - 1))

    gain = one(*split[0])
    for cut in split[1:]:
        gain = gain * one(*cut)
    return gain


def centred(own_key, extent, deviation, most, cuts=(), kind=jnp.bfloat16):
    entries = jax.random.normal(own_key, extent, jnp.float32) * deviation
    if len(cuts) > 0:
        entries = block_scale(own_key, extent, cuts, -0.22, 0.18) * entries
    return jnp.clip(entries, min=-most, max=most).astype(kind)


def setup_inputs(seed: int = 0) -> dict:
    arg_keys = jax.random.split(jax.random.key(seed), 4)
    return {
        "noise": centred(arg_keys[0], (NZ, NX, NY), 1.0, 6.0, ((1, 128),), jnp.float32),
        "kappa": jnp.clip(jnp.exp(math.log(2.0) - 3.6888794 * jax.random.uniform(arg_keys[1], (NZ, NX, NY), jnp.float32) ** block_scale(arg_keys[1], (NZ, NX, NY), ((1, 8), (2, 16)), -0.2, 0.2)), 0.05, 2.0),
        "mask": touch_ends((jax.random.randint(arg_keys[2], (NX, NY), 0, 4) < 3).astype(jnp.int32), jax.random.fold_in(arg_keys[2], 1), 0, 1),
    }


def neighbours(padded):
    centre = padded[:, 1:-1, 1:-1]
    with_ends = jnp.pad(centre, ((1, 1), (0, 0), (0, 0)))
    total = padded[:, 2:, 1:-1] + padded[:, :-2, 1:-1]
    total = total + padded[:, 1:-1, 2:] + padded[:, 1:-1, :-2]
    return total + with_ends[2:] + with_ends[:-2]


def factors(kappa):
    pivots = []
    for layer_index in range(kappa.shape[0]):
        diagonal = 2.5 + kappa[layer_index]
        if layer_index > 0:
            diagonal = diagonal - pivots[-1]
        pivots.append(1.0 / diagonal)
    return pivots


def thomas(field, pivots):
    layers = field.shape[0]
    forward = []
    for layer_index in range(layers):
        current = field[layer_index]
        if layer_index > 0:
            current = current + forward[-1]
        forward.append(current * pivots[layer_index])
    result = [None] * layers
    solved = forward[layers - 1]
    result[layers - 1] = solved
    for layer_index in range(layers - 2, -1, -1):
        solved = forward[layer_index] + pivots[layer_index] * solved
        result[layer_index] = solved
    return jnp.stack(result, 0)


def reference(noise, kappa, mask):
    inverse = mask[None].astype(jnp.float32) / (6.0 + kappa)
    field = inverse * noise
    for repeat in range(2):
        padded = jnp.pad(field, ((0, 0), (1, 1), (1, 1)))
        field = inverse * (noise + neighbours(padded))
    return thomas(field, factors(kappa))
```

```python
import functools

import jax
import jax.numpy as jnp
from jax import lax
from jax.experimental import pallas as pl
from jax.experimental.pallas import tpu as pltpu
from jax.sharding import PartitionSpec as P

MESH = pl.DeviceIdType.MESH
F32 = jnp.float32
NL = 16
SR = 16
BC = 256
TOP = 16
EARLY = 4


def wait_bytes(ref, sem):
    pltpu.make_async_copy(ref, ref, sem).wait()


def kernel(na, nd, noise, kappa, mask, out, *scratch):
    (strip, kap, msk, noise_x, inv_x, init_x, mid_x, fwd, rows_send, rowi_send, rown, rowi, q_send, qn, qi, qp,
     e_send, e_recv, load_sem, bulk_send, bulk_recv, q_ssem, q_rsem, r_ssem, r_rsem, qh_ssem, qh_rsem,
     e_ssem, e_rsem, i_ssem, i_rsem, c_ssem, c_rsem, out_sem) = scratch
    br = nd * SR
    end = TOP + br
    a, d = lax.axis_index("ax"), lax.axis_index("ay")
    above, below = lax.rem(a + na - 1, na), lax.rem(a + 1, na)
    left, right = lax.rem(d + nd - 1, nd), lax.rem(d + 1, nd)

    loads = [
        pltpu.make_async_copy(noise, strip, load_sem.at[0]),
        pltpu.make_async_copy(kappa, kap, load_sem.at[1]),
        pltpu.make_async_copy(mask, msk, load_sem.at[2]),
    ]
    for load in loads:
        load.start()

    barrier = pltpu.get_barrier_semaphore()

    def greet(x, y):
        pl.semaphore_signal(barrier, inc=1, device_id=(x, y), device_id_type=MESH)

    @pl.loop(1, nd)
    def _(k):
        greet(a, lax.rem(d + k, nd))

    for x in (above, below):
        for y in (d, left, right):
            greet(x, y)
    greet(above, nd - 1)
    greet(below, 0)
    edge = jnp.where(d == 0, nd, 0) + jnp.where(d == nd - 1, nd, 0)
    pl.semaphore_wait(barrier, nd - 1 + 6 + edge)

    def bulk(layer):
        pltpu.make_async_copy(
            noise.at[layer, :, pl.ds(pl.multiple_of(d * BC, BC), BC)],
            noise_x.at[layer, pl.ds(pl.multiple_of(TOP + d * SR, SR), SR), :],
            bulk_recv.at[layer],
        ).start()

        @pl.loop(1, nd)
        def _(k):
            t = lax.rem(d + k, nd)
            pltpu.make_async_remote_copy(
                src_ref=noise.at[layer, :, pl.ds(pl.multiple_of(t * BC, BC), BC)],
                dst_ref=noise_x.at[layer, pl.ds(pl.multiple_of(TOP + d * SR, SR), SR), :],
                send_sem=bulk_send.at[layer],
                recv_sem=bulk_recv.at[layer],
                device_id=(a, t),
                device_id_type=MESH,
            ).start()

    @pl.loop(0, EARLY)
    def _(layer):
        bulk(layer)

    lane = lax.broadcasted_iota(jnp.int32, (SR, 128), 1)
    sub = lax.broadcasted_iota(jnp.int32, (8, BC), 0)

    loads[0].wait()

    @pl.loop(0, nd)
    def _(t):
        before = pl.multiple_of(lax.rem(t + nd - 1, nd) * BC + 128, 128)
        after = pl.multiple_of(lax.rem(t + 1, nd) * BC, 128)
        packed = jnp.zeros((SR, 128), F32)
        for layer in range(NL):
            both = jnp.where(lane < 64, strip[layer, :, pl.ds(after, 128)], strip[layer, :, pl.ds(before, 128)])
            packed = jnp.where(lane // 4 == layer, pltpu.roll(both, (4 * layer + 2) % 128, 1), packed)
        q_send[t] = packed

    def q_place(s):
        return qn.at[pl.ds(pl.multiple_of(TOP + s * SR, SR), SR), :]

    pltpu.make_async_copy(q_send.at[d], q_place(d), q_rsem).start()

    @pl.loop(1, nd)
    def _(k):
        t = lax.rem(d + k, nd)
        pltpu.make_async_remote_copy(
            src_ref=q_send.at[t], dst_ref=q_place(d), send_sem=q_ssem, recv_sem=q_rsem,
            device_id=(a, t), device_id_type=MESH,
        ).start()

    def pick_rows(tile, first, i):
        return pltpu.roll(tile, (2 * i - first) % 8, 0)

    def send_rows(first_row, first, x, slot, q_src, q_dst):
        @pl.loop(0, nd)
        def _(t):
            cols = pl.ds(pl.multiple_of(t * BC, BC), BC)
            for q in range(NL // 4):
                packed = jnp.zeros((8, BC), F32)
                for i in range(4):
                    tile = strip[4 * q + i, first_row:first_row + 8, cols]
                    packed = jnp.where(sub // 2 == i, pick_rows(tile, first, i), packed)
                rows_send[q, :, cols] = packed
            pltpu.make_async_remote_copy(
                src_ref=rows_send.at[:, :, cols], dst_ref=rown.at[slot], send_sem=r_ssem, recv_sem=r_rsem.at[slot],
                device_id=(x, t), device_id_type=MESH,
            ).start()
            pltpu.make_async_remote_copy(
                src_ref=q_send.at[t, q_src:q_src + 8, :], dst_ref=qn.at[q_dst:q_dst + 8, :], send_sem=qh_ssem,
                recv_sem=qh_rsem.at[slot], device_id=(x, t), device_id_type=MESH,
            ).start()

    @pl.when(d == 0)
    def _():
        send_rows(0, 0, above, 1, 0, end)

    @pl.when(d == nd - 1)
    def _():
        send_rows(SR - 8, 6, below, 0, SR - 8, TOP - 8)

    loads[1].wait()
    loads[2].wait()
    rb = 32
    lane_b = lax.broadcasted_iota(jnp.int32, (rb, 128), 1)

    @pl.loop(0, br // rb)
    def _(b):
        rows = pl.ds(pl.multiple_of(b * rb, rb), rb)
        active = msk[rows, :].astype(F32)
        packed = jnp.zeros((rb, 128), F32)
        for layer in range(NL):
            inverse = active / (6.0 + kap[layer, rows, :])
            inv_x[layer, pl.ds(pl.multiple_of(TOP + b * rb, 16), rb), :] = inverse
            both = jnp.where(lane_b < 64, inverse[:, :128], inverse[:, 128:])
            packed = jnp.where(lane_b // 4 == layer, pltpu.roll(both, (4 * layer + 2) % 128, 1), packed)
        e_send[rows, :] = packed

    halos = []
    for slot, y in ((0, right), (1, left)):
        halos.append(pltpu.make_async_remote_copy(
            src_ref=e_send, dst_ref=e_recv.at[slot, TOP:end, :], send_sem=e_ssem.at[slot], recv_sem=e_rsem.at[slot],
            device_id=(a, y), device_id_type=MESH,
        ))
        halos.append(pltpu.make_async_remote_copy(
            src_ref=e_send.at[br - 8:br, :], dst_ref=e_recv.at[slot, TOP - 8:TOP, :], send_sem=c_ssem.at[slot, 0],
            recv_sem=c_rsem.at[slot, 0], device_id=(below, y), device_id_type=MESH,
        ))
        halos.append(pltpu.make_async_remote_copy(
            src_ref=e_send.at[0:8, :], dst_ref=e_recv.at[slot, end:end + 8, :], send_sem=c_ssem.at[slot, 1],
            recv_sem=c_rsem.at[slot, 1], device_id=(above, y), device_id_type=MESH,
        ))
    for q in range(NL // 4):
        down = jnp.zeros((8, BC), F32)
        up = jnp.zeros((8, BC), F32)
        for i in range(4):
            layer = 4 * q + i
            down = jnp.where(sub // 2 == i, pick_rows(inv_x[layer, end - 8:end, :], 6, i), down)
            up = jnp.where(sub // 2 == i, pick_rows(inv_x[layer, TOP:TOP + 8, :], 0, i), up)
        rowi_send[0, q] = down
        rowi_send[1, q] = up
    for slot, x in ((0, below), (1, above)):
        halos.append(pltpu.make_async_remote_copy(
            src_ref=rowi_send.at[slot], dst_ref=rowi.at[slot], send_sem=i_ssem.at[slot], recv_sem=i_rsem.at[slot],
            device_id=(x, d), device_id_type=MESH,
        ))
    for halo in halos:
        halo.start()

    @pl.loop(EARLY, NL)
    def _(layer):
        bulk(layer)

    @pl.loop(0, br // rb)
    def _(b):
        rows = pl.ds(pl.multiple_of(b * rb, rb), rb)
        pivot = jnp.zeros((rb, BC), F32)
        for layer in range(NL):
            pivot = 1.0 / (2.5 + kap[layer, rows, :] - pivot)
            kap[layer, rows, :] = pivot

    @pl.loop(0, (br + 16) // 16)
    def _(b):
        rows = pl.ds(pl.multiple_of(8 + b * 16, 8), 16)
        for field in (init_x, mid_x):
            for layer in (0, NL + 1):
                field[layer, rows, :] = jnp.zeros((16, BC + 128), F32)

    @pl.loop(0, br // 16)
    def _(b):
        fwd[0, pl.ds(pl.multiple_of(b * 16, 16), 16), :] = jnp.zeros((16, BC), F32)

    for halo in halos:
        halo.wait()
    for slot in range(2):
        wait_bytes(rown.at[slot], r_rsem.at[slot])
        place = (TOP - 8, end)[slot]
        wait_bytes(qn.at[place:place + 8, :], qh_rsem.at[slot])
    wait_bytes(qn.at[TOP:end, :], q_rsem)
    keep_top = jnp.where(a > 0, 1.0, 0.0).astype(F32)
    keep_end = jnp.where(a < na - 1, 1.0, 0.0).astype(F32)
    keep_left = jnp.where(d > 0, 1.0, 0.0).astype(F32)
    keep_right = jnp.where(d < nd - 1, 1.0, 0.0).astype(F32)

    @pl.loop(0, NL // 4)
    def _(q):
        for i in range(4):
            layer = 4 * q + i
            inv_x[layer, TOP - 8:TOP, :] = keep_top * pltpu.roll(rowi[0, q], (6 - 2 * i) % 8, 0)
            inv_x[layer, end:end + 8, :] = keep_end * pltpu.roll(rowi[1, q], (-2 * i) % 8, 0)
            noise_x[layer, TOP - 8:TOP, :] = pltpu.roll(rown[0, q], (6 - 2 * i) % 8, 0)
            noise_x[layer, end:end + 8, :] = pltpu.roll(rown[1, q], (-2 * i) % 8, 0)

    lane8 = lax.broadcasted_iota(jnp.int32, (8, 128), 1)

    @pl.loop(0, (br + 16) // 8)
    def _(b):
        rows = pl.ds(pl.multiple_of(8 + b * 8, 8), 8)
        keep = jnp.where(b == 0, keep_top, jnp.where(b == (br + 16) // 8 - 1, keep_end, 1.0))
        inverse = jnp.where(lane8 % 4 < 2, e_recv[0, rows, :] * (keep * keep_left), e_recv[1, rows, :] * (keep * keep_right))
        qi[rows, :] = inverse
        qp[rows, :] = inverse * qn[rows, :]

    def sideways(field):
        return pltpu.roll(field, 1, 1) + pltpu.roll(field, BC + 127, 1)

    def around(field, layer, first):
        near = field[layer + 1, pl.ds(first - 8, 32), :]
        rows = pl.ds(first, 16)
        return near[7:23] + near[9:25] + sideways(near[8:24]) + field[layer, rows, :] + field[layer + 2, rows, :]

    def initial(layer):
        turn = lax.rem(254 - 4 * layer, 128)

        @pl.loop(0, (br + 16) // 16)
        def _(b):
            rows = pl.ds(pl.multiple_of(8 + b * 16, 8), 16)
            init_x[layer + 1, rows, :BC] = inv_x[layer, rows, :] * noise_x[layer, rows, :]
            init_x[layer + 1, rows, BC:] = pltpu.roll(qp[rows, :], turn, 1)

    def middle(layer):
        turn = lax.rem(254 - 4 * layer, 128)

        @pl.loop(0, (br + 16) // 16)
        def _(b):
            first = pl.multiple_of(8 + b * 16, 8)
            rows = pl.ds(first, 16)
            total = around(init_x, layer, first)
            mid_x[layer + 1, rows, :BC] = inv_x[layer, rows, :] * (noise_x[layer, rows, :] + total[:, :BC])
            mid_x[layer + 1, rows, BC:] = pltpu.roll(qi[rows, :], turn, 1) * (pltpu.roll(qn[rows, :], turn, 1) + total[:, BC:])

    def smooth(layer):
        @pl.loop(0, br // 16)
        def _(b):
            first = pl.multiple_of(TOP + b * 16, 16)
            rows = pl.ds(first, 16)
            own = pl.ds(pl.multiple_of(b * 16, 16), 16)
            total = around(mid_x, layer, first)[:, :BC]
            field = inv_x[layer, rows, :] * (noise_x[layer, rows, :] + total)
            fwd[layer + 1, own, :] = (field + fwd[layer, own, :]) * kap[layer, own, :]

    @pl.loop(0, NL + 2)
    def _(step):
        @pl.when(step < NL)
        def _():
            wait_bytes(noise_x.at[step, TOP:end, :], bulk_recv.at[step])
            initial(step)

        @pl.when((step >= 1) & (step <= NL))
        def _():
            middle(step - 1)

        @pl.when(step >= 2)
        def _():
            smooth(step - 2)

    def result(b):
        rows = pl.ds(pl.multiple_of(b * rb, rb), rb)
        return pltpu.make_async_copy(fwd.at[1:NL + 1, rows, :], out.at[:, rows, :], out_sem.at[b])

    @pl.loop(0, br // rb)
    def _(b):
        rows = pl.ds(pl.multiple_of(b * rb, rb), rb)
        solved = fwd[NL, rows, :]
        for layer in range(NL - 2, -1, -1):
            solved = fwd[layer + 1, rows, :] + kap[layer, rows, :] * solved
            fwd[layer + 1, rows, :] = solved
        result(b).start()

    @pl.loop(0, NL)
    def _(layer):
        wait_bytes(noise.at[layer, :, :(nd - 1) * BC], bulk_send.at[layer])

    wait_bytes(q_send.at[:nd - 1], q_ssem)

    @pl.when((d == 0) | (d == nd - 1))
    def _():
        wait_bytes(rows_send, r_ssem)
        wait_bytes(q_send.at[:, 0:8, :], qh_ssem)

    @pl.loop(0, br // rb)
    def _(b):
        result(b).wait()


def body(noise, kappa, mask):
    na, nd = lax.axis_size("ax"), lax.axis_size("ay")
    br = nd * SR
    ext = br + 2 * TOP
    dma = pltpu.SemaphoreType.DMA
    scratch = [
        pltpu.VMEM((NL, SR, nd * BC), F32),
        pltpu.VMEM((NL, br, BC), F32),
        pltpu.VMEM((br, BC), jnp.int32),
        pltpu.VMEM((NL, ext, BC), F32),
        pltpu.VMEM((NL, ext, BC), F32),
        pltpu.VMEM((NL + 2, ext, BC + 128), F32),
        pltpu.VMEM((NL + 2, ext, BC + 128), F32),
        pltpu.VMEM((NL + 1, br, BC), F32),
        pltpu.VMEM((NL // 4, 8, nd * BC), F32),
        pltpu.VMEM((2, NL // 4, 8, BC), F32),
        pltpu.VMEM((2, NL // 4, 8, BC), F32),
        pltpu.VMEM((2, NL // 4, 8, BC), F32),
        pltpu.VMEM((nd, SR, 128), F32),
        pltpu.VMEM((ext, 128), F32),
        pltpu.VMEM((ext, 128), F32),
        pltpu.VMEM((ext, 128), F32),
        pltpu.VMEM((br, 128), F32),
        pltpu.VMEM((2, ext, 128), F32),
        dma((3,)), dma((NL,)), dma((NL,)),
        dma, dma,
        dma, dma((2,)),
        dma, dma((2,)),
        dma((2,)), dma((2,)),
        dma((2,)), dma((2,)),
        dma((2, 2)), dma((2, 2)),
        dma((br // 32,)),
    ]
    return pl.pallas_call(
        functools.partial(kernel, na, nd),
        out_shape=jax.ShapeDtypeStruct((NL, br, BC), F32),
        in_specs=[pl.BlockSpec(memory_space=pl.ANY)] * 3,
        out_specs=pl.BlockSpec(memory_space=pl.ANY),
        scratch_shapes=scratch,
        compiler_params=pltpu.CompilerParams(collective_id=0, has_side_effects=True, vmem_limit_bytes=60 << 20),
        name="sweeps",
    )(noise, kappa, mask)


def solution(mesh):
    in_specs = (P(None, ("ax", "ay"), None), P(None, "ax", "ay"), P("ax", "ay"))
    out_specs = P(None, "ax", "ay")
    return jax.shard_map(body, mesh=mesh, in_specs=in_specs, out_specs=out_specs, check_vma=False)
```

```python
import functools

import jax
import jax.numpy as jnp
from jax import lax
from jax.experimental import pallas as pl
from jax.experimental.pallas import tpu as pltpu
from jax.sharding import PartitionSpec as P

MESH = pl.DeviceIdType.MESH
F32 = jnp.float32
NL = 16
SR = 16
BC = 256
TOP = 16
UG = 17
US = 16
RB = 32
EARLY = 4


def wait_bytes(ref, sem):
    pltpu.make_async_copy(ref, ref, sem).wait()


def kernel(na, nd, noise, kappa, mask, fwd, kap, *scratch):
    (strip, msk, noise_x, inv_x, init_x, mid_x, rows_send, rowi_send, rown, rowi, q_send, qn, qi, qp, h_init, h_mid,
     e_send, e_recv, load_sem, bulk_send, bulk_recv, q_ssem, q_rsem, r_ssem, r_rsem, qh_ssem, qh_rsem,
     e_ssem, e_rsem, i_ssem, i_rsem, c_ssem, c_rsem) = scratch
    br = nd * SR
    end = TOP + br
    a, d = lax.axis_index("ax"), lax.axis_index("ay")
    above, below = lax.rem(a + na - 1, na), lax.rem(a + 1, na)
    left, right = lax.rem(d + nd - 1, nd), lax.rem(d + 1, nd)

    loads = [
        pltpu.make_async_copy(noise, strip, load_sem.at[0]),
        pltpu.make_async_copy(kappa, kap, load_sem.at[1]),
        pltpu.make_async_copy(mask, msk, load_sem.at[2]),
    ]
    for load in loads:
        load.start()

    barrier = pltpu.get_barrier_semaphore()

    def greet(x, y):
        pl.semaphore_signal(barrier, inc=1, device_id=(x, y), device_id_type=MESH)

    @pl.loop(1, nd)
    def _(k):
        greet(a, lax.rem(d + k, nd))

    for x in (above, below):
        for y in (d, left, right):
            greet(x, y)
    greet(above, nd - 1)
    greet(below, 0)
    edge = jnp.where(d == 0, nd, 0) + jnp.where(d == nd - 1, nd, 0)
    pl.semaphore_wait(barrier, nd - 1 + 6 + edge)

    def bulk(layer):
        pltpu.make_async_copy(
            noise.at[layer, :, pl.ds(pl.multiple_of(d * BC, BC), BC)],
            noise_x.at[layer, pl.ds(pl.multiple_of(TOP + d * SR, SR), SR), :],
            bulk_recv.at[layer],
        ).start()

        @pl.loop(1, nd)
        def _(k):
            t = lax.rem(d + k, nd)
            pltpu.make_async_remote_copy(
                src_ref=noise.at[layer, :, pl.ds(pl.multiple_of(t * BC, BC), BC)],
                dst_ref=noise_x.at[layer, pl.ds(pl.multiple_of(TOP + d * SR, SR), SR), :],
                send_sem=bulk_send.at[layer],
                recv_sem=bulk_recv.at[layer],
                device_id=(a, t),
                device_id_type=MESH,
            ).start()

    @pl.loop(0, EARLY)
    def _(layer):
        bulk(layer)

    lane = lax.broadcasted_iota(jnp.int32, (SR, 128), 1)
    sub = lax.broadcasted_iota(jnp.int32, (8, BC), 0)

    loads[0].wait()

    @pl.loop(0, nd)
    def _(t):
        before = pl.multiple_of(lax.rem(t + nd - 1, nd) * BC + 128, 128)
        here = pl.multiple_of(t * BC, BC)
        after = pl.multiple_of(lax.rem(t + 1, nd) * BC, 128)
        packed = jnp.zeros((SR, 128), F32)
        for layer in range(NL):
            low = jnp.where(lane < 64, strip[layer, :, pl.ds(here, 128)], strip[layer, :, pl.ds(before, 128)])
            high = jnp.where(lane < 64, strip[layer, :, pl.ds(after, 128)], strip[layer, :, pl.ds(here + 128, 128)])
            low = pltpu.roll(low, (8 * layer + 2) % 128, 1)
            high = pltpu.roll(high, (8 * layer + 5) % 128, 1)
            packed = jnp.where(lane // 8 == layer, jnp.where(lane % 8 < 4, low, high), packed)
        q_send[t] = packed

    def q_place(s):
        return qn.at[pl.ds(pl.multiple_of(TOP + s * SR, SR), SR), :]

    pltpu.make_async_copy(q_send.at[d], q_place(d), q_rsem).start()

    @pl.loop(1, nd)
    def _(k):
        t = lax.rem(d + k, nd)
        pltpu.make_async_remote_copy(
            src_ref=q_send.at[t], dst_ref=q_place(d), send_sem=q_ssem, recv_sem=q_rsem,
            device_id=(a, t), device_id_type=MESH,
        ).start()

    def pick_rows(tile, first, i):
        return pltpu.roll(tile, (2 * i - first) % 8, 0)

    def send_rows(first_row, first, x, slot, q_src, q_dst):
        @pl.loop(0, nd)
        def _(t):
            cols = pl.ds(pl.multiple_of(t * BC, BC), BC)
            for q in range(NL // 4):
                packed = jnp.zeros((8, BC), F32)
                for i in range(4):
                    tile = strip[4 * q + i, first_row:first_row + 8, cols]
                    packed = jnp.where(sub // 2 == i, pick_rows(tile, first, i), packed)
                rows_send[q, :, cols] = packed
            pltpu.make_async_remote_copy(
                src_ref=rows_send.at[:, :, cols], dst_ref=rown.at[slot], send_sem=r_ssem, recv_sem=r_rsem.at[slot],
                device_id=(x, t), device_id_type=MESH,
            ).start()
            pltpu.make_async_remote_copy(
                src_ref=q_send.at[t, q_src:q_src + 8, :], dst_ref=qn.at[q_dst:q_dst + 8, :], send_sem=qh_ssem,
                recv_sem=qh_rsem.at[slot], device_id=(x, t), device_id_type=MESH,
            ).start()

    @pl.when(d == 0)
    def _():
        send_rows(0, 0, above, 1, 0, end)

    @pl.when(d == nd - 1)
    def _():
        send_rows(SR - 8, 6, below, 0, SR - 8, TOP - 8)

    loads[1].wait()
    loads[2].wait()
    rb = 32
    lane_b = lax.broadcasted_iota(jnp.int32, (rb, 128), 1)

    @pl.loop(0, br // rb)
    def _(b):
        rows = pl.ds(pl.multiple_of(b * rb, rb), rb)
        active = msk[rows, :].astype(F32)
        packed = jnp.zeros((rb, 128), F32)
        for layer in range(NL):
            inverse = active / (6.0 + kap[layer, rows, :])
            inv_x[layer, pl.ds(pl.multiple_of(TOP + b * rb, 16), rb), :] = inverse
            both = jnp.where(lane_b < 64, inverse[:, :128], inverse[:, 128:])
            low = pltpu.roll(both, (8 * layer + 2) % 128, 1)
            high = pltpu.roll(both, (8 * layer + 5) % 128, 1)
            packed = jnp.where(lane_b // 8 == layer, jnp.where(lane_b % 8 < 3, low, high), packed)
        e_send[rows, :] = packed

    halos = []
    for slot, y in ((0, right), (1, left)):
        halos.append(pltpu.make_async_remote_copy(
            src_ref=e_send, dst_ref=e_recv.at[slot, TOP:end, :], send_sem=e_ssem.at[slot], recv_sem=e_rsem.at[slot],
            device_id=(a, y), device_id_type=MESH,
        ))
        halos.append(pltpu.make_async_remote_copy(
            src_ref=e_send.at[br - 8:br, :], dst_ref=e_recv.at[slot, TOP - 8:TOP, :], send_sem=c_ssem.at[slot, 0],
            recv_sem=c_rsem.at[slot, 0], device_id=(below, y), device_id_type=MESH,
        ))
        halos.append(pltpu.make_async_remote_copy(
            src_ref=e_send.at[0:8, :], dst_ref=e_recv.at[slot, end:end + 8, :], send_sem=c_ssem.at[slot, 1],
            recv_sem=c_rsem.at[slot, 1], device_id=(above, y), device_id_type=MESH,
        ))
    for q in range(NL // 4):
        down = jnp.zeros((8, BC), F32)
        up = jnp.zeros((8, BC), F32)
        for i in range(4):
            layer = 4 * q + i
            down = jnp.where(sub // 2 == i, pick_rows(inv_x[layer, end - 8:end, :], 6, i), down)
            up = jnp.where(sub // 2 == i, pick_rows(inv_x[layer, TOP:TOP + 8, :], 0, i), up)
        rowi_send[0, q] = down
        rowi_send[1, q] = up
    for slot, x in ((0, below), (1, above)):
        halos.append(pltpu.make_async_remote_copy(
            src_ref=rowi_send.at[slot], dst_ref=rowi.at[slot], send_sem=i_ssem.at[slot], recv_sem=i_rsem.at[slot],
            device_id=(x, d), device_id_type=MESH,
        ))
    for halo in halos:
        halo.start()

    @pl.loop(EARLY, NL)
    def _(layer):
        bulk(layer)

    @pl.loop(0, br // rb)
    def _(b):
        rows = pl.ds(pl.multiple_of(b * rb, rb), rb)
        pivot = jnp.zeros((rb, BC), F32)
        for layer in range(NL):
            pivot = 1.0 / (2.5 + kap[layer, rows, :] - pivot)
            kap[layer, rows, :] = pivot

    @pl.loop(0, (br + 16) // 16)
    def _(b):
        rows = pl.ds(pl.multiple_of(8 + b * 16, 8), 16)
        for field in (init_x, mid_x):
            for layer in (0, NL + 1):
                for c in range(2):
                    field[layer, c, rows, :] = jnp.zeros((16, 128), F32)

    for halo in halos:
        halo.wait()
    for slot in range(2):
        wait_bytes(rown.at[slot], r_rsem.at[slot])
        place = (TOP - 8, end)[slot]
        wait_bytes(qn.at[place:place + 8, :], qh_rsem.at[slot])
    wait_bytes(qn.at[TOP:end, :], q_rsem)
    keep_top = jnp.where(a > 0, 1.0, 0.0).astype(F32)
    keep_end = jnp.where(a < na - 1, 1.0, 0.0).astype(F32)
    keep_left = jnp.where(d > 0, 1.0, 0.0).astype(F32)
    keep_right = jnp.where(d < nd - 1, 1.0, 0.0).astype(F32)

    @pl.loop(0, NL // 4)
    def _(q):
        for i in range(4):
            layer = 4 * q + i
            inv_x[layer, TOP - 8:TOP, :] = keep_top * pltpu.roll(rowi[0, q], (6 - 2 * i) % 8, 0)
            inv_x[layer, end:end + 8, :] = keep_end * pltpu.roll(rowi[1, q], (-2 * i) % 8, 0)
            noise_x[layer, TOP - 8:TOP, :] = pltpu.roll(rown[0, q], (6 - 2 * i) % 8, 0)
            noise_x[layer, end:end + 8, :] = pltpu.roll(rown[1, q], (-2 * i) % 8, 0)

    groups = (br + 16) // 8
    lane8 = lax.broadcasted_iota(jnp.int32, (8, 128), 1)
    place8 = lane8 % 8

    def beside(packed):
        return jnp.where(place8 == 3, pltpu.roll(packed, 126, 1), pltpu.roll(packed, 3, 1))

    @pl.loop(0, groups)
    def _(b):
        rows = pl.ds(pl.multiple_of(8 + b * 8, 8), 8)
        own = pl.ds(pl.multiple_of(lax.min(lax.max(b - 1, 0), br // 8 - 1) * 8, 8), 8)
        keep = jnp.where(b == 0, keep_top, jnp.where(b == groups - 1, keep_end, 1.0))
        outer = jnp.where(place8 < 2, e_recv[0, rows, :] * (keep * keep_left), e_recv[1, rows, :] * (keep * keep_right))
        inverse = jnp.where((place8 >= 2) & (place8 < 5), e_send[own, :], outer)
        first = inverse * qn[rows, :]
        qi[rows, :] = inverse
        qp[rows, :] = first
        h_init[rows, :] = beside(first)

    @pl.loop(0, br // 8)
    def _(b):
        first = pl.multiple_of(TOP + b * 8, 8)
        rows = pl.ds(first, 8)
        here = qp[rows, :]
        total = qp[pl.ds(first - 1, 8), :] + qp[pl.ds(first + 1, 8), :]
        total = total + pltpu.roll(here, 1, 1) + pltpu.roll(here, 127, 1)
        total = total + jnp.where(lane8 < 8, 0.0, pltpu.roll(here, 8, 1))
        total = total + jnp.where(lane8 >= 120, 0.0, pltpu.roll(here, 120, 1))
        h_mid[rows, :] = beside(qi[rows, :] * (qn[rows, :] + total))

    lane_l = lane8 == 0
    lane_r = lane8 == 127

    def sums(field, layer, turn, halo, first):
        rows = pl.ds(first, 8)
        outer = pltpu.roll(halo[rows, :], turn, 1)
        here = [field[layer + 1, c, rows, :] for c in range(2)]
        back = [pltpu.roll(x, 1, 1) for x in here]
        fore = [pltpu.roll(x, 127, 1) for x in here]
        side = [
            jnp.where(lane_l, outer, back[0]) + jnp.where(lane_r, fore[1], fore[0]),
            jnp.where(lane_l, back[0], back[1]) + jnp.where(lane_r, outer, fore[1]),
        ]
        return [
            side[c] + (field[layer + 1, c, pl.ds(first - 1, 8), :] + field[layer + 1, c, pl.ds(first + 1, 8), :])
            + (field[layer, c, rows, :] + field[layer + 2, c, rows, :])
            for c in range(2)
        ]

    def initial(layer):
        @pl.loop(0, groups // UG)
        def _(b):
            for g in range(UG):
                rows = pl.ds(pl.multiple_of(8 + (b * UG + g) * 8, 8), 8)
                for c in range(2):
                    cols = slice(c * 128, c * 128 + 128)
                    init_x[layer + 1, c, rows, :] = inv_x[layer, rows, cols] * noise_x[layer, rows, cols]

    def middle(layer):
        turn = lax.rem(252 - 8 * layer, 128)

        @pl.loop(0, groups // UG)
        def _(b):
            for g in range(UG):
                first = pl.multiple_of(8 + (b * UG + g) * 8, 8)
                rows = pl.ds(first, 8)
                total = sums(init_x, layer, turn, h_init, first)
                for c in range(2):
                    cols = slice(c * 128, c * 128 + 128)
                    mid_x[layer + 1, c, rows, :] = inv_x[layer, rows, cols] * (noise_x[layer, rows, cols] + total[c])

    def smooth(layer):
        turn = lax.rem(252 - 8 * layer, 128)
        before = lax.max(layer - 1, 0)
        keep = jnp.where(layer == 0, 0.0, 1.0).astype(F32)

        @pl.loop(0, br // 8 // US)
        def _(b):
            for g in range(US):
                own = pl.multiple_of((b * US + g) * 8, 8)
                first = pl.multiple_of(TOP + own, 8)
                rows = pl.ds(first, 8)
                total = sums(mid_x, layer, turn, h_mid, first)
                for c in range(2):
                    cols = slice(c * 128, c * 128 + 128)
                    field = inv_x[layer, rows, cols] * (noise_x[layer, rows, cols] + total[c])
                    previous = fwd[before, pl.ds(own, 8), cols] * keep
                    fwd[layer, pl.ds(own, 8), cols] = (field + previous) * kap[layer, pl.ds(own, 8), cols]

    @pl.loop(0, br // 8)
    def _(b):
        fwd[0, pl.ds(pl.multiple_of(b * 8, 8), 8), :] = jnp.zeros((8, BC), F32)

    @pl.loop(0, NL + 2)
    def _(step):
        @pl.when(step < NL)
        def _():
            wait_bytes(noise_x.at[step, TOP:end, :], bulk_recv.at[step])
            initial(step)

        @pl.when((step >= 1) & (step <= NL))
        def _():
            middle(step - 1)

        @pl.when(step >= 2)
        def _():
            smooth(step - 2)

    @pl.loop(0, NL)
    def _(layer):
        wait_bytes(noise.at[layer, :, :(nd - 1) * BC], bulk_send.at[layer])

    wait_bytes(q_send.at[:nd - 1], q_ssem)

    @pl.when((d == 0) | (d == nd - 1))
    def _():
        wait_bytes(rows_send, r_ssem)
        wait_bytes(q_send.at[:, 0:8, :], qh_ssem)


def back_kernel(fwd, pivots, out):
    rows = pl.ds(pl.multiple_of(pl.program_id(0) * RB, RB), RB)
    solved = fwd[NL - 1, rows, :]
    out[NL - 1] = solved
    for layer in range(NL - 2, -1, -1):
        solved = fwd[layer, rows, :] + pivots[layer, rows, :] * solved
        out[layer] = solved


def body(noise, kappa, mask):
    na, nd = lax.axis_size("ax"), lax.axis_size("ay")
    br = nd * SR
    ext = br + 2 * TOP
    dma = pltpu.SemaphoreType.DMA
    scratch = [
        pltpu.VMEM((NL, SR, nd * BC), F32),
        pltpu.VMEM((br, BC), jnp.int32),
        pltpu.VMEM((NL, ext, BC), F32),
        pltpu.VMEM((NL, ext, BC), F32),
        pltpu.VMEM((NL + 2, 2, ext, 128), F32),
        pltpu.VMEM((NL + 2, 2, ext, 128), F32),
        pltpu.VMEM((NL // 4, 8, nd * BC), F32),
        pltpu.VMEM((2, NL // 4, 8, BC), F32),
        pltpu.VMEM((2, NL // 4, 8, BC), F32),
        pltpu.VMEM((2, NL // 4, 8, BC), F32),
        pltpu.VMEM((nd, SR, 128), F32),
        pltpu.VMEM((ext, 128), F32),
        pltpu.VMEM((ext, 128), F32),
        pltpu.VMEM((ext, 128), F32),
        pltpu.VMEM((ext, 128), F32),
        pltpu.VMEM((ext, 128), F32),
        pltpu.VMEM((br, 128), F32),
        pltpu.VMEM((2, ext, 128), F32),
        dma((3,)), dma((NL,)), dma((NL,)),
        dma, dma,
        dma, dma((2,)),
        dma, dma((2,)),
        dma((2,)), dma((2,)),
        dma((2,)), dma((2,)),
        dma((2, 2)), dma((2, 2)),
    ]
    field = pltpu.VMEM((NL, br, BC), F32)
    forward, pivots = pl.pallas_call(
        functools.partial(kernel, na, nd),
        out_shape=(field, field),
        in_specs=[pl.BlockSpec(memory_space=pltpu.HBM)] * 3,
        out_specs=[pl.BlockSpec(memory_space=pltpu.VMEM)] * 2,
        scratch_shapes=scratch,
        compiler_params=pltpu.CompilerParams(collective_id=0, has_side_effects=True, vmem_limit_bytes=48 << 20),
        name="sweeps",
    )(noise, kappa, mask)
    return pl.pallas_call(
        back_kernel,
        grid=(br // RB,),
        out_shape=jax.ShapeDtypeStruct((NL, br, BC), F32),
        in_specs=[pl.BlockSpec(memory_space=pltpu.VMEM)] * 2,
        out_specs=pl.BlockSpec((NL, RB, BC), lambda b: (0, b, 0)),
        compiler_params=pltpu.CompilerParams(vmem_limit_bytes=16 << 20),
        name="back",
    )(forward, pivots)


def solution(mesh):
    in_specs = (P(None, ("ax", "ay"), None), P(None, "ax", "ay"), P("ax", "ay"))
    out_specs = P(None, "ax", "ay")
    return jax.shard_map(body, mesh=mesh, in_specs=in_specs, out_specs=out_specs, check_vma=False)
```

```python
import functools

import jax
import jax.numpy as jnp
from jax import lax
from jax.experimental import pallas as pl
from jax.experimental.pallas import tpu as pltpu
from jax.sharding import PartitionSpec as P

MESH = pl.DeviceIdType.MESH
F32 = jnp.float32
NL = 16
SR = 16
BC = 256
TOP = 16
LAG = 2
RB = 32
EARLY = 4


def wait_bytes(ref, sem):
    pltpu.make_async_copy(ref, ref, sem).wait()


def kernel(na, nd, noise, kappa, mask, fwd, kap, *scratch):
    (strip, msk, noise_x, inv_x, init_x, mid_x, mid_h, rows_send, rowi_send, rown, rowi, q_send, q_recv, qn, qp,
     h_init, h_mid, h_inv, e_send, f_send, f_recv, c_recv, load_sem, bulk_send, bulk_recv, q_ssem, q_rsem, r_ssem, r_rsem, qh_ssem, qh_rsem,
     e_ssem, e_rsem, i_ssem, i_rsem, c_ssem, c_rsem) = scratch
    br = nd * SR
    end = TOP + br
    a, d = lax.axis_index("ax"), lax.axis_index("ay")
    above, below = lax.rem(a + na - 1, na), lax.rem(a + 1, na)
    left, right = lax.rem(d + nd - 1, nd), lax.rem(d + 1, nd)

    loads = [
        pltpu.make_async_copy(noise, strip, load_sem.at[0]),
        pltpu.make_async_copy(kappa, kap, load_sem.at[1]),
        pltpu.make_async_copy(mask, msk, load_sem.at[2]),
    ]
    for load in loads:
        load.start()

    barrier = pltpu.get_barrier_semaphore()

    def greet(x, y):
        pl.semaphore_signal(barrier, inc=1, device_id=(x, y), device_id_type=MESH)

    @pl.loop(1, nd)
    def _(k):
        greet(a, lax.rem(d + k, nd))

    for x in (above, below):
        for y in (d, left, right):
            greet(x, y)
    greet(above, nd - 1)
    greet(below, 0)
    edge = jnp.where(d == 0, nd, 0) + jnp.where(d == nd - 1, nd, 0)
    pl.semaphore_wait(barrier, nd - 1 + 6 + edge)

    def bulk(layer):
        pltpu.make_async_copy(
            noise.at[layer, :, pl.ds(pl.multiple_of(d * BC, BC), BC)],
            noise_x.at[layer, pl.ds(pl.multiple_of(TOP + d * SR, SR), SR), :],
            bulk_recv.at[layer],
        ).start()

        @pl.loop(1, nd)
        def _(k):
            t = lax.rem(d + k, nd)
            pltpu.make_async_remote_copy(
                src_ref=noise.at[layer, :, pl.ds(pl.multiple_of(t * BC, BC), BC)],
                dst_ref=noise_x.at[layer, pl.ds(pl.multiple_of(TOP + d * SR, SR), SR), :],
                send_sem=bulk_send.at[layer],
                recv_sem=bulk_recv.at[layer],
                device_id=(a, t),
                device_id_type=MESH,
            ).start()

    @pl.loop(0, EARLY)
    def _(layer):
        bulk(layer)

    lane = lax.broadcasted_iota(jnp.int32, (8, 128), 1)
    sub = lax.broadcasted_iota(jnp.int32, (8, BC), 0)

    loads[0].wait()

    @pl.loop(0, nd)
    def _(t):
        before = pl.multiple_of(lax.rem(t + nd - 1, nd) * BC + 128, 128)
        after = pl.multiple_of(lax.rem(t + 1, nd) * BC, 128)
        packed = jnp.zeros((8, 128), F32)
        for layer in range(NL):
            for half in range(2):
                rows = slice(half * 8, half * 8 + 8)
                both = jnp.where(lane < 64, strip[layer, rows, pl.ds(after, 128)], strip[layer, rows, pl.ds(before, 128)])
                packed = jnp.where(lane // 4 == layer + 16 * half, pltpu.roll(both, (4 * layer + 2 + 64 * half) % 128, 1), packed)
        q_send[t] = packed

    def q_place(s):
        return q_recv.at[s + 1]

    pltpu.make_async_copy(q_send.at[d], q_place(d), q_rsem).start()

    @pl.loop(1, nd)
    def _(k):
        t = lax.rem(d + k, nd)
        pltpu.make_async_remote_copy(
            src_ref=q_send.at[t], dst_ref=q_place(d), send_sem=q_ssem, recv_sem=q_rsem,
            device_id=(a, t), device_id_type=MESH,
        ).start()

    def pick_rows(tile, first, i):
        return pltpu.roll(tile, (2 * i - first) % 8, 0)

    def send_rows(first_row, first, x, slot):
        @pl.loop(0, nd)
        def _(t):
            cols = pl.ds(pl.multiple_of(t * BC, BC), BC)
            for q in range(NL // 4):
                packed = jnp.zeros((8, BC), F32)
                for i in range(4):
                    tile = strip[4 * q + i, first_row:first_row + 8, cols]
                    packed = jnp.where(sub // 2 == i, pick_rows(tile, first, i), packed)
                rows_send[q, :, cols] = packed
            pltpu.make_async_remote_copy(
                src_ref=rows_send.at[:, :, cols], dst_ref=rown.at[slot], send_sem=r_ssem, recv_sem=r_rsem.at[slot],
                device_id=(x, t), device_id_type=MESH,
            ).start()
            pltpu.make_async_remote_copy(
                src_ref=q_send.at[t], dst_ref=q_recv.at[(0, nd + 1)[slot]], send_sem=qh_ssem,
                recv_sem=qh_rsem.at[slot], device_id=(x, t), device_id_type=MESH,
            ).start()

    @pl.when(d == 0)
    def _():
        send_rows(0, 0, above, 1)

    @pl.when(d == nd - 1)
    def _():
        send_rows(SR - 8, 6, below, 0)

    loads[1].wait()
    loads[2].wait()
    rb = 32
    lane_b = lax.broadcasted_iota(jnp.int32, (rb, 128), 1)

    @pl.loop(0, br // rb)
    def _(b):
        rows = pl.ds(pl.multiple_of(b * rb, rb), rb)
        active = msk[rows, :].astype(F32)
        packed = jnp.zeros((rb, 128), F32)
        for layer in range(NL):
            inverse = active / (6.0 + kap[layer, rows, :])
            inv_x[layer, pl.ds(pl.multiple_of(TOP + b * rb, 16), rb), :] = inverse
            both = jnp.where(lane_b < 64, inverse[:, :128], inverse[:, 128:])
            packed = jnp.where(lane_b // 4 == layer, pltpu.roll(both, (4 * layer + 2) % 128, 1), packed)
        e_send[rows, :] = packed

    folds = ((0, 2, 64, 66), (0, 126, 64, 62))
    fr = br // 4
    place = lane % 4

    @pl.loop(0, fr // 8)
    def _(b):
        for slot in range(2):
            packed = jnp.zeros((8, 128), F32)
            for k in range(4):
                piece = pltpu.roll(e_send[pl.ds(pl.multiple_of(k * fr + b * 8, 8), 8), :], folds[slot][k], 1)
                low = (0, 2, 0, 2)[k] if slot == 0 else (2, 0, 2, 0)[k]
                mine = (place >= low) & (place < low + 2) & (lane // 64 == k // 2)
                packed = jnp.where(mine, piece, packed)
            f_send[slot, pl.ds(pl.multiple_of(b * 8, 8), 8), :] = packed

    halos = []
    for slot, y in ((0, right), (1, left)):
        halos.append(pltpu.make_async_remote_copy(
            src_ref=f_send.at[slot], dst_ref=f_recv.at[slot], send_sem=e_ssem.at[slot], recv_sem=e_rsem.at[slot],
            device_id=(a, y), device_id_type=MESH,
        ))
        halos.append(pltpu.make_async_remote_copy(
            src_ref=e_send.at[br - 8:br, :], dst_ref=c_recv.at[slot, 0], send_sem=c_ssem.at[slot, 0],
            recv_sem=c_rsem.at[slot, 0], device_id=(below, y), device_id_type=MESH,
        ))
        halos.append(pltpu.make_async_remote_copy(
            src_ref=e_send.at[0:8, :], dst_ref=c_recv.at[slot, 1], send_sem=c_ssem.at[slot, 1],
            recv_sem=c_rsem.at[slot, 1], device_id=(above, y), device_id_type=MESH,
        ))
    for q in range(NL // 4):
        down = jnp.zeros((8, BC), F32)
        up = jnp.zeros((8, BC), F32)
        for i in range(4):
            layer = 4 * q + i
            down = jnp.where(sub // 2 == i, pick_rows(inv_x[layer, end - 8:end, :], 6, i), down)
            up = jnp.where(sub // 2 == i, pick_rows(inv_x[layer, TOP:TOP + 8, :], 0, i), up)
        rowi_send[0, q] = down
        rowi_send[1, q] = up
    for slot, x in ((0, below), (1, above)):
        halos.append(pltpu.make_async_remote_copy(
            src_ref=rowi_send.at[slot], dst_ref=rowi.at[slot], send_sem=i_ssem.at[slot], recv_sem=i_rsem.at[slot],
            device_id=(x, d), device_id_type=MESH,
        ))
    for halo in halos:
        halo.start()

    @pl.loop(EARLY, NL)
    def _(layer):
        bulk(layer)

    @pl.loop(0, br // rb)
    def _(b):
        rows = pl.ds(pl.multiple_of(b * rb, rb), rb)
        pivot = jnp.zeros((rb, BC), F32)
        for layer in range(NL):
            pivot = 1.0 / (2.5 + kap[layer, rows, :] - pivot)
            kap[layer, rows, :] = pivot

    @pl.loop(0, (br + 16) // 16)
    def _(b):
        rows = pl.ds(pl.multiple_of(8 + b * 16, 8), 16)
        for field in (init_x, mid_x):
            for layer in (0, NL + 1):
                for c in range(2):
                    field[layer, c, rows, :] = jnp.zeros((16, 128), F32)

    for halo in halos:
        halo.wait()
    for slot in range(2):
        wait_bytes(rown.at[slot], r_rsem.at[slot])
        wait_bytes(q_recv.at[slot], qh_rsem.at[slot])
    wait_bytes(q_recv.at[1:nd + 1], q_rsem)
    keep_top = jnp.where(a > 0, 1.0, 0.0).astype(F32)
    keep_end = jnp.where(a < na - 1, 1.0, 0.0).astype(F32)
    keep_left = jnp.where(d > 0, 1.0, 0.0).astype(F32)
    keep_right = jnp.where(d < nd - 1, 1.0, 0.0).astype(F32)

    @pl.loop(0, NL // 4)
    def _(q):
        for i in range(4):
            layer = 4 * q + i
            inv_x[layer, TOP - 8:TOP, :] = keep_top * pltpu.roll(rowi[0, q], (6 - 2 * i) % 8, 0)
            inv_x[layer, end:end + 8, :] = keep_end * pltpu.roll(rowi[1, q], (-2 * i) % 8, 0)
            noise_x[layer, TOP - 8:TOP, :] = pltpu.roll(rown[0, q], (6 - 2 * i) % 8, 0)
            noise_x[layer, end:end + 8, :] = pltpu.roll(rown[1, q], (-2 * i) % 8, 0)

    groups = (br + 16) // 8

    def beside(packed):
        return jnp.where(place == 1, pltpu.roll(packed, 127, 1), pltpu.roll(packed, 1, 1))

    def sides(first, from_left, from_right, noise_q):
        rows = pl.ds(first, 8)
        inverse = jnp.where(place < 2, from_left * keep_left, from_right * keep_right)
        qn[rows, :] = noise_q
        qp[rows, :] = inverse * noise_q
        h_inv[rows, :] = inverse

    sides(TOP - 8, c_recv[0, 0] * keep_top, c_recv[1, 0] * keep_top, pltpu.roll(q_recv[0], 64, 1))
    sides(end, c_recv[0, 1] * keep_end, c_recv[1, 1] * keep_end, q_recv[nd + 1])
    for k in range(4):
        @pl.loop(0, fr // SR)
        def _(b):
            noise_q = q_recv[1 + k * (fr // SR) + b]
            for half in range(2):
                rows = pl.ds(pl.multiple_of(b * SR + half * 8, 8), 8)
                pieces = [pltpu.roll(f_recv[slot, rows, :], (128 - folds[slot][k]) % 128, 1) for slot in range(2)]
                first = pl.multiple_of(TOP + k * fr + b * SR + half * 8, 8)
                sides(first, *pieces, pltpu.roll(noise_q, 64, 1) if half else noise_q)

    @pl.loop(0, br // 8)
    def _(b):
        first = pl.multiple_of(TOP + b * 8, 8)
        rows = pl.ds(first, 8)
        here = qp[rows, :]
        total = qp[pl.ds(first - 1, 8), :] + qp[pl.ds(first + 1, 8), :]
        total = total + jnp.where(place < 2, pltpu.roll(here, 1, 1), pltpu.roll(here, 127, 1))
        total = total + jnp.where(lane < 4, 0.0, pltpu.roll(here, 4, 1))
        total = total + jnp.where(lane >= 60, 0.0, pltpu.roll(here, 124, 1))
        inverse = h_inv[rows, :]
        h_mid[rows, :] = beside(inverse * (qn[rows, :] + total))
        h_inv[rows, :] = beside(inverse)

    @pl.loop(0, groups)
    def _(b):
        rows = pl.ds(pl.multiple_of(8 + b * 8, 8), 8)
        h_init[rows, :] = beside(qp[rows, :])

    @pl.loop(0, br // 8)
    def _(b):
        fwd[0, pl.ds(pl.multiple_of(b * 8, 8), 8), :] = jnp.zeros((8, BC), F32)

    lane_l = lane == 0
    lane_r = lane == 127
    cols = (slice(0, 128), slice(128, 256))

    def around(field, layer, first, here, outer):
        rows = pl.ds(first, 8)
        back = [pltpu.roll(x, 1, 1) for x in here]
        fore = [pltpu.roll(x, 127, 1) for x in here]
        side = (
            jnp.where(lane_l, outer, back[0]) + jnp.where(lane_r, fore[1], fore[0]),
            jnp.where(lane_l, back[0], back[1]) + jnp.where(lane_r, outer, fore[1]),
        )
        return [
            side[c] + (field[layer + 1, c, pl.ds(first - 1, 8), :] + field[layer + 1, c, pl.ds(first + 1, 8), :])
            + field[layer, c, rows, :]
            for c in range(2)
        ]

    def group(step, first, do_initial, do_middle, do_smooth):
        rows = pl.ds(first, 8)
        stores = []
        initial = middle = None
        if do_initial:
            initial = [inv_x[step, rows, cols[c]] * noise_x[step, rows, cols[c]] for c in range(2)]
            stores += [(init_x, (step + 1, c, rows, slice(None)), initial[c]) for c in range(2)]
        if do_middle:
            layer = step - 1
            turn = lax.rem(254 - 4 * layer, 128)
            here = [init_x[layer + 1, c, rows, :] for c in range(2)]
            total = around(init_x, layer, first, here, pltpu.roll(h_init[rows, :], turn, 1))
            if initial is not None:
                total = [total[c] + initial[c] for c in range(2)]
            middle = [inv_x[layer, rows, cols[c]] * (noise_x[layer, rows, cols[c]] + total[c]) for c in range(2)]
            inner = jnp.where(lane < 64, here[0], here[1])
            outer = pltpu.roll(h_mid[rows, :], turn, 1) + pltpu.roll(h_inv[rows, :], turn, 1) * inner
            stores += [(mid_x, (layer + 1, c, rows, slice(None)), middle[c]) for c in range(2)]
            stores += [(mid_h, (layer, rows, slice(None)), outer)]
        if do_smooth:
            layer = step - 2
            own = pl.ds(pl.multiple_of(first - TOP, 8), 8)
            here = [mid_x[layer + 1, c, rows, :] for c in range(2)]
            total = around(mid_x, layer, first, here, mid_h[layer, rows, :])
            if middle is not None:
                total = [total[c] + middle[c] for c in range(2)]
            for c in range(2):
                field = inv_x[layer, rows, cols[c]] * (noise_x[layer, rows, cols[c]] + total[c])
                previous = fwd[lax.max(layer - 1, 0), own, cols[c]]
                pivot = kap[layer, own, cols[c]]
                stores += [(fwd, (layer, own, cols[c]), (field + previous) * pivot)]
        return stores

    def sweep(step, do_initial, do_middle, do_smooth):
        pending = []
        low, high = (0, groups) if do_middle else (1, groups - 1)
        for g in range(low, high):
            pending.append(group(step, 8 + 8 * g, do_initial, do_middle, do_smooth and 1 <= g < groups - 1))
            if len(pending) > LAG:
                for ref, index, value in pending.pop(0):
                    ref[index] = value
        for stores in pending:
            for ref, index, value in stores:
                ref[index] = value

    for step in range(2):
        wait_bytes(noise_x.at[step, TOP:end, :], bulk_recv.at[step])

        @pl.loop(0, groups)
        def _(b):
            for ref, index, value in group(step, pl.multiple_of(8 + b * 8, 8), True, step > 0, False):
                ref[index] = value

    @pl.loop(2, NL)
    def _(step):
        wait_bytes(noise_x.at[step, TOP:end, :], bulk_recv.at[step])
        sweep(step, True, True, True)

    sweep(NL, False, True, True)
    sweep(NL + 1, False, False, True)

    @pl.loop(0, NL)
    def _(layer):
        wait_bytes(noise.at[layer, :, :(nd - 1) * BC], bulk_send.at[layer])

    wait_bytes(q_send.at[:nd - 1], q_ssem)

    @pl.when((d == 0) | (d == nd - 1))
    def _():
        wait_bytes(rows_send, r_ssem)
        wait_bytes(q_send, qh_ssem)


def back_kernel(fwd, pivots, out, solution_x, out_sem):
    def result(b):
        rows = pl.ds(pl.multiple_of(b * RB, RB), RB)
        return pltpu.make_async_copy(solution_x.at[:, rows, :], out.at[:, rows, :], out_sem.at[b])

    steps = fwd.shape[1] // RB

    @pl.loop(0, steps)
    def _(b):
        rows = pl.ds(pl.multiple_of(b * RB, RB), RB)
        solved = fwd[NL - 1, rows, :]
        solution_x[NL - 1, rows, :] = solved
        for layer in range(NL - 2, -1, -1):
            solved = fwd[layer, rows, :] + pivots[layer, rows, :] * solved
            solution_x[layer, rows, :] = solved
        result(b).start()

    @pl.loop(0, steps)
    def _(b):
        result(b).wait()


def body(noise, kappa, mask):
    na, nd = lax.axis_size("ax"), lax.axis_size("ay")
    br = nd * SR
    ext = br + 2 * TOP
    dma = pltpu.SemaphoreType.DMA
    scratch = [
        pltpu.VMEM((NL, SR, nd * BC), F32),
        pltpu.VMEM((br, BC), jnp.int32),
        pltpu.VMEM((NL, ext, BC), F32),
        pltpu.VMEM((NL, ext, BC), F32),
        pltpu.VMEM((NL + 2, 2, ext, 128), F32),
        pltpu.VMEM((NL + 2, 2, ext, 128), F32),
        pltpu.VMEM((NL, ext, 128), F32),
        pltpu.VMEM((NL // 4, 8, nd * BC), F32),
        pltpu.VMEM((2, NL // 4, 8, BC), F32),
        pltpu.VMEM((2, NL // 4, 8, BC), F32),
        pltpu.VMEM((2, NL // 4, 8, BC), F32),
        pltpu.VMEM((nd, 8, 128), F32),
        pltpu.VMEM((nd + 2, 8, 128), F32),
        pltpu.VMEM((ext, 128), F32),
        pltpu.VMEM((ext, 128), F32),
        pltpu.VMEM((ext, 128), F32),
        pltpu.VMEM((ext, 128), F32),
        pltpu.VMEM((ext, 128), F32),
        pltpu.VMEM((br, 128), F32),
        pltpu.VMEM((2, br // 4, 128), F32),
        pltpu.VMEM((2, br // 4, 128), F32),
        pltpu.VMEM((2, 2, 8, 128), F32),
        dma((3,)), dma((NL,)), dma((NL,)),
        dma, dma,
        dma, dma((2,)),
        dma, dma((2,)),
        dma((2,)), dma((2,)),
        dma((2,)), dma((2,)),
        dma((2, 2)), dma((2, 2)),
    ]
    field = pltpu.VMEM((NL, br, BC), F32)
    forward, pivots = pl.pallas_call(
        functools.partial(kernel, na, nd),
        out_shape=(field, field),
        in_specs=[pl.BlockSpec(memory_space=pltpu.HBM)] * 3,
        out_specs=[pl.BlockSpec(memory_space=pltpu.VMEM)] * 2,
        scratch_shapes=scratch,
        compiler_params=pltpu.CompilerParams(collective_id=0, has_side_effects=True, vmem_limit_bytes=48 << 20),
        name="sweeps",
    )(noise, kappa, mask)
    return pl.pallas_call(
        back_kernel,
        out_shape=jax.ShapeDtypeStruct((NL, br, BC), F32),
        in_specs=[pl.BlockSpec(memory_space=pltpu.VMEM)] * 2,
        out_specs=pl.BlockSpec(memory_space=pltpu.HBM),
        scratch_shapes=[field, dma((br // RB,))],
        compiler_params=pltpu.CompilerParams(vmem_limit_bytes=16 << 20),
        name="back",
    )(forward, pivots)


def solution(mesh):
    in_specs = (P(None, ("ax", "ay"), None), P(None, "ax", "ay"), P("ax", "ay"))
    out_specs = P(None, "ax", "ay")
    return jax.shard_map(body, mesh=mesh, in_specs=in_specs, out_specs=out_specs, check_vma=False)
```

```python
import functools

import jax
import jax.numpy as jnp
from jax import lax
from jax.experimental import pallas as pl
from jax.experimental.pallas import tpu as pltpu
from jax.sharding import PartitionSpec as P

MESH = pl.DeviceIdType.MESH
F32 = jnp.float32
NL = 16
SR = 16
BC = 256
TOP = 16
LAG = 2
RB = 32
EARLY = 4


def wait_bytes(ref, sem):
    pltpu.make_async_copy(ref, ref, sem).wait()


def kernel(na, nd, noise, kappa, mask, fwd, kap, *scratch):
    (strip, msk, noise_x, inv_x, init_x, mid_x, mid_h, rows_send, rowi_send, rown, rowi, q_send, q_recv, qn, qp,
     h_init, h_mid, h_inv, e_send, f_send, f_recv, c_recv, load_sem, bulk_send, bulk_recv, q_ssem, q_rsem, r_ssem, r_rsem, qh_ssem, qh_rsem,
     e_ssem, e_rsem, i_ssem, i_rsem, c_ssem, c_rsem) = scratch
    br = nd * SR
    end = TOP + br
    a, d = lax.axis_index("ax"), lax.axis_index("ay")
    above, below = lax.rem(a + na - 1, na), lax.rem(a + 1, na)
    left, right = lax.rem(d + nd - 1, nd), lax.rem(d + 1, nd)

    loads = [
        pltpu.make_async_copy(noise, strip, load_sem.at[0]),
        pltpu.make_async_copy(kappa, kap, load_sem.at[1]),
        pltpu.make_async_copy(mask, msk, load_sem.at[2]),
    ]
    for load in loads:
        load.start()

    barrier = pltpu.get_barrier_semaphore()

    def greet(x, y):
        pl.semaphore_signal(barrier, inc=1, device_id=(x, y), device_id_type=MESH)

    @pl.loop(1, nd)
    def _(k):
        greet(a, lax.rem(d + k, nd))

    edge = jnp.where(d == 0, nd, 0) + jnp.where(d == nd - 1, nd, 0)
    odd = lax.rem(a, 2)

    @pl.when(odd == 0)
    def _():
        @pl.loop(0, nd)
        def _(k):
            greet(above, lax.rem(d + k, nd))
            greet(below, lax.rem(d + k, nd))

    pl.semaphore_wait(barrier, nd - 1 + odd * (2 * nd))

    @pl.when(odd == 1)
    def _():
        for x in (above, below):
            for y in (d, left, right):
                greet(x, y)
        greet(above, nd - 1)
        greet(below, 0)
        for y, x in ((0, above), (nd - 1, below)):
            @pl.when(d == y)
            def _():
                @pl.loop(0, nd)
                def _(t):
                    greet(x, t)

    def bulk(layer):
        pltpu.make_async_copy(
            noise.at[layer, :, pl.ds(pl.multiple_of(d * BC, BC), BC)],
            noise_x.at[layer, pl.ds(pl.multiple_of(TOP + d * SR, SR), SR), :],
            bulk_recv.at[layer],
        ).start()

        @pl.loop(1, nd)
        def _(k):
            t = lax.rem(d + k, nd)
            pltpu.make_async_remote_copy(
                src_ref=noise.at[layer, :, pl.ds(pl.multiple_of(t * BC, BC), BC)],
                dst_ref=noise_x.at[layer, pl.ds(pl.multiple_of(TOP + d * SR, SR), SR), :],
                send_sem=bulk_send,
                recv_sem=bulk_recv.at[layer],
                device_id=(a, t),
                device_id_type=MESH,
            ).start()

    @pl.loop(0, EARLY)
    def _(layer):
        bulk(layer)

    lane = lax.broadcasted_iota(jnp.int32, (8, 128), 1)
    sub = lax.broadcasted_iota(jnp.int32, (8, BC), 0)

    loads[0].wait()

    @pl.loop(0, nd)
    def _(t):
        before = pl.multiple_of(lax.rem(t + nd - 1, nd) * BC + 128, 128)
        after = pl.multiple_of(lax.rem(t + 1, nd) * BC, 128)
        packed = jnp.zeros((8, 128), F32)
        for layer in range(NL):
            for half in range(2):
                rows = slice(half * 8, half * 8 + 8)
                both = jnp.where(lane < 64, strip[layer, rows, pl.ds(after, 128)], strip[layer, rows, pl.ds(before, 128)])
                packed = jnp.where(lane // 4 == layer + 16 * half, pltpu.roll(both, (4 * layer + 2 + 64 * half) % 128, 1), packed)
        q_send[t] = packed

    def q_place(s):
        return q_recv.at[s + 1]

    pltpu.make_async_copy(q_send.at[d], q_place(d), q_rsem).start()

    @pl.loop(1, nd)
    def _(k):
        t = lax.rem(d + k, nd)
        pltpu.make_async_remote_copy(
            src_ref=q_send.at[t], dst_ref=q_place(d), send_sem=q_ssem, recv_sem=q_rsem,
            device_id=(a, t), device_id_type=MESH,
        ).start()

    def pick_rows(tile, first, i):
        return pltpu.roll(tile, (2 * i - first) % 8, 0)

    def send_rows(first_row, first, x, slot):
        @pl.loop(0, nd)
        def _(t):
            cols = pl.ds(pl.multiple_of(t * BC, BC), BC)
            for q in range(NL // 4):
                packed = jnp.zeros((8, BC), F32)
                for i in range(4):
                    tile = strip[4 * q + i, first_row:first_row + 8, cols]
                    packed = jnp.where(sub // 2 == i, pick_rows(tile, first, i), packed)
                rows_send[q, :, cols] = packed
            pltpu.make_async_remote_copy(
                src_ref=rows_send.at[:, :, cols], dst_ref=rown.at[slot], send_sem=r_ssem, recv_sem=r_rsem.at[slot],
                device_id=(x, t), device_id_type=MESH,
            ).start()
            pltpu.make_async_remote_copy(
                src_ref=q_send.at[t], dst_ref=q_recv.at[(0, nd + 1)[slot]], send_sem=qh_ssem,
                recv_sem=qh_rsem.at[slot], device_id=(x, t), device_id_type=MESH,
            ).start()

    @pl.when(odd == 0)
    def _():
        pl.semaphore_wait(barrier, 8 + edge)

    @pl.when(d == 0)
    def _():
        send_rows(0, 0, above, 1)

    @pl.when(d == nd - 1)
    def _():
        send_rows(SR - 8, 6, below, 0)

    loads[1].wait()
    loads[2].wait()
    rb = 32
    lane_b = lax.broadcasted_iota(jnp.int32, (rb, 128), 1)

    @pl.loop(0, br // rb)
    def _(b):
        rows = pl.ds(pl.multiple_of(b * rb, rb), rb)
        active = msk[rows, :].astype(F32)
        packed = jnp.zeros((rb, 128), F32)
        for layer in range(NL):
            inverse = active / (6.0 + kap[layer, rows, :])
            inv_x[layer, pl.ds(pl.multiple_of(TOP + b * rb, 16), rb), :] = inverse
            both = jnp.where(lane_b < 64, inverse[:, :128], inverse[:, 128:])
            packed = jnp.where(lane_b // 4 == layer, pltpu.roll(both, (4 * layer + 2) % 128, 1), packed)
        e_send[rows, :] = packed

    folds = ((0, 2, 64, 66), (0, 126, 64, 62))
    fr = br // 4
    place = lane % 4

    @pl.loop(0, fr // 8)
    def _(b):
        for slot in range(2):
            packed = jnp.zeros((8, 128), F32)
            for k in range(4):
                piece = pltpu.roll(e_send[pl.ds(pl.multiple_of(k * fr + b * 8, 8), 8), :], folds[slot][k], 1)
                low = (0, 2, 0, 2)[k] if slot == 0 else (2, 0, 2, 0)[k]
                mine = (place >= low) & (place < low + 2) & (lane // 64 == k // 2)
                packed = jnp.where(mine, piece, packed)
            f_send[slot, pl.ds(pl.multiple_of(b * 8, 8), 8), :] = packed

    halos = []
    for slot, y in ((0, right), (1, left)):
        halos.append(pltpu.make_async_remote_copy(
            src_ref=f_send.at[slot], dst_ref=f_recv.at[slot], send_sem=e_ssem.at[slot], recv_sem=e_rsem.at[slot],
            device_id=(a, y), device_id_type=MESH,
        ))
        halos.append(pltpu.make_async_remote_copy(
            src_ref=e_send.at[br - 8:br, :], dst_ref=c_recv.at[slot, 0], send_sem=c_ssem.at[slot, 0],
            recv_sem=c_rsem.at[slot, 0], device_id=(below, y), device_id_type=MESH,
        ))
        halos.append(pltpu.make_async_remote_copy(
            src_ref=e_send.at[0:8, :], dst_ref=c_recv.at[slot, 1], send_sem=c_ssem.at[slot, 1],
            recv_sem=c_rsem.at[slot, 1], device_id=(above, y), device_id_type=MESH,
        ))
    for q in range(NL // 4):
        down = jnp.zeros((8, BC), F32)
        up = jnp.zeros((8, BC), F32)
        for i in range(4):
            layer = 4 * q + i
            down = jnp.where(sub // 2 == i, pick_rows(inv_x[layer, end - 8:end, :], 6, i), down)
            up = jnp.where(sub // 2 == i, pick_rows(inv_x[layer, TOP:TOP + 8, :], 0, i), up)
        rowi_send[0, q] = down
        rowi_send[1, q] = up
    for slot, x in ((0, below), (1, above)):
        halos.append(pltpu.make_async_remote_copy(
            src_ref=rowi_send.at[slot], dst_ref=rowi.at[slot], send_sem=i_ssem.at[slot], recv_sem=i_rsem.at[slot],
            device_id=(x, d), device_id_type=MESH,
        ))
    for halo in halos:
        halo.start()

    @pl.loop(EARLY, NL)
    def _(layer):
        bulk(layer)

    @pl.loop(0, br // rb)
    def _(b):
        rows = pl.ds(pl.multiple_of(b * rb, rb), rb)
        pivot = jnp.zeros((rb, BC), F32)
        for layer in range(NL):
            pivot = 1.0 / (2.5 + kap[layer, rows, :] - pivot)
            kap[layer, rows, :] = pivot

    @pl.loop(0, (br + 16) // 16)
    def _(b):
        rows = pl.ds(pl.multiple_of(8 + b * 16, 8), 16)
        for field in (init_x, mid_x):
            for layer in (0, NL + 1):
                for c in range(2):
                    field[layer, c, rows, :] = jnp.zeros((16, 128), F32)

    for halo in halos:
        halo.wait()
    for slot in range(2):
        wait_bytes(rown.at[slot], r_rsem.at[slot])
        wait_bytes(q_recv.at[slot], qh_rsem.at[slot])
    wait_bytes(q_recv.at[1:nd + 1], q_rsem)
    keep_top = jnp.where(a > 0, 1.0, 0.0).astype(F32)
    keep_end = jnp.where(a < na - 1, 1.0, 0.0).astype(F32)
    keep_left = jnp.where(d > 0, 1.0, 0.0).astype(F32)
    keep_right = jnp.where(d < nd - 1, 1.0, 0.0).astype(F32)

    @pl.loop(0, NL // 4)
    def _(q):
        for i in range(4):
            layer = 4 * q + i
            inv_x[layer, TOP - 8:TOP, :] = keep_top * pltpu.roll(rowi[0, q], (6 - 2 * i) % 8, 0)
            inv_x[layer, end:end + 8, :] = keep_end * pltpu.roll(rowi[1, q], (-2 * i) % 8, 0)
            noise_x[layer, TOP - 8:TOP, :] = pltpu.roll(rown[0, q], (6 - 2 * i) % 8, 0)
            noise_x[layer, end:end + 8, :] = pltpu.roll(rown[1, q], (-2 * i) % 8, 0)

    groups = (br + 16) // 8

    def beside(packed):
        return jnp.where(place == 1, pltpu.roll(packed, 127, 1), pltpu.roll(packed, 1, 1))

    def sides(first, from_left, from_right, noise_q):
        rows = pl.ds(first, 8)
        inverse = jnp.where(place < 2, from_left * keep_left, from_right * keep_right)
        qn[rows, :] = noise_q
        qp[rows, :] = inverse * noise_q
        h_inv[rows, :] = inverse

    sides(TOP - 8, c_recv[0, 0] * keep_top, c_recv[1, 0] * keep_top, pltpu.roll(q_recv[0], 64, 1))
    sides(end, c_recv[0, 1] * keep_end, c_recv[1, 1] * keep_end, q_recv[nd + 1])
    for k in range(4):
        @pl.loop(0, fr // SR)
        def _(b):
            noise_q = q_recv[1 + k * (fr // SR) + b]
            for half in range(2):
                rows = pl.ds(pl.multiple_of(b * SR + half * 8, 8), 8)
                pieces = [pltpu.roll(f_recv[slot, rows, :], (128 - folds[slot][k]) % 128, 1) for slot in range(2)]
                first = pl.multiple_of(TOP + k * fr + b * SR + half * 8, 8)
                sides(first, *pieces, pltpu.roll(noise_q, 64, 1) if half else noise_q)

    @pl.loop(0, br // 8)
    def _(b):
        first = pl.multiple_of(TOP + b * 8, 8)
        rows = pl.ds(first, 8)
        here = qp[rows, :]
        total = qp[pl.ds(first - 1, 8), :] + qp[pl.ds(first + 1, 8), :]
        total = total + jnp.where(place < 2, pltpu.roll(here, 1, 1), pltpu.roll(here, 127, 1))
        total = total + jnp.where(lane < 4, 0.0, pltpu.roll(here, 4, 1))
        total = total + jnp.where(lane >= 60, 0.0, pltpu.roll(here, 124, 1))
        inverse = h_inv[rows, :]
        h_mid[rows, :] = beside(inverse * (qn[rows, :] + total))
        h_inv[rows, :] = beside(inverse)

    @pl.loop(0, groups)
    def _(b):
        rows = pl.ds(pl.multiple_of(8 + b * 8, 8), 8)
        h_init[rows, :] = beside(qp[rows, :])

    @pl.loop(0, br // 8)
    def _(b):
        fwd[0, pl.ds(pl.multiple_of(b * 8, 8), 8), :] = jnp.zeros((8, BC), F32)

    lane_l = lane == 0
    lane_r = lane == 127
    cols = (slice(0, 128), slice(128, 256))

    def around(field, layer, first, here, outer):
        rows = pl.ds(first, 8)
        back = [pltpu.roll(x, 1, 1) for x in here]
        fore = [pltpu.roll(x, 127, 1) for x in here]
        side = (
            jnp.where(lane_l, outer, back[0]) + jnp.where(lane_r, fore[1], fore[0]),
            jnp.where(lane_l, back[0], back[1]) + jnp.where(lane_r, outer, fore[1]),
        )
        return [
            side[c] + (field[layer + 1, c, pl.ds(first - 1, 8), :] + field[layer + 1, c, pl.ds(first + 1, 8), :])
            + field[layer, c, rows, :]
            for c in range(2)
        ]

    def group(step, first, do_initial, do_middle, do_smooth):
        rows = pl.ds(first, 8)
        stores = []
        initial = middle = None
        if do_initial:
            initial = [inv_x[step, rows, cols[c]] * noise_x[step, rows, cols[c]] for c in range(2)]
            stores += [(init_x, (step + 1, c, rows, slice(None)), initial[c]) for c in range(2)]
        if do_middle:
            layer = step - 1
            turn = lax.rem(254 - 4 * layer, 128)
            here = [init_x[layer + 1, c, rows, :] for c in range(2)]
            total = around(init_x, layer, first, here, pltpu.roll(h_init[rows, :], turn, 1))
            if initial is not None:
                total = [total[c] + initial[c] for c in range(2)]
            middle = [inv_x[layer, rows, cols[c]] * (noise_x[layer, rows, cols[c]] + total[c]) for c in range(2)]
            inner = jnp.where(lane < 64, here[0], here[1])
            outer = pltpu.roll(h_mid[rows, :], turn, 1) + pltpu.roll(h_inv[rows, :], turn, 1) * inner
            stores += [(mid_x, (layer + 1, c, rows, slice(None)), middle[c]) for c in range(2)]
            stores += [(mid_h, (layer, rows, slice(None)), outer)]
        if do_smooth:
            layer = step - 2
            own = pl.ds(pl.multiple_of(first - TOP, 8), 8)
            here = [mid_x[layer + 1, c, rows, :] for c in range(2)]
            total = around(mid_x, layer, first, here, mid_h[layer, rows, :])
            if middle is not None:
                total = [total[c] + middle[c] for c in range(2)]
            for c in range(2):
                field = inv_x[layer, rows, cols[c]] * (noise_x[layer, rows, cols[c]] + total[c])
                previous = fwd[lax.max(layer - 1, 0), own, cols[c]]
                pivot = kap[layer, own, cols[c]]
                stores += [(fwd, (layer, own, cols[c]), (field + previous) * pivot)]
        return stores

    def sweep(step, do_initial, do_middle, do_smooth):
        pending = []
        low, high = (0, groups) if do_middle else (1, groups - 1)
        for g in range(low, high):
            pending.append(group(step, 8 + 8 * g, do_initial, do_middle, do_smooth and 1 <= g < groups - 1))
            if len(pending) > LAG:
                for ref, index, value in pending.pop(0):
                    ref[index] = value
        for stores in pending:
            for ref, index, value in stores:
                ref[index] = value

    for step in range(2):
        wait_bytes(noise_x.at[step, TOP:end, :], bulk_recv.at[step])

        @pl.loop(0, groups)
        def _(b):
            for ref, index, value in group(step, pl.multiple_of(8 + b * 8, 8), True, step > 0, False):
                ref[index] = value

    @pl.loop(2, NL)
    def _(step):
        wait_bytes(noise_x.at[step, TOP:end, :], bulk_recv.at[step])
        sweep(step, True, True, True)

    sweep(NL, False, True, True)
    sweep(NL + 1, False, False, True)

    wait_bytes(noise.at[:, :, :(nd - 1) * BC], bulk_send)

    wait_bytes(q_send.at[:nd - 1], q_ssem)

    @pl.when((d == 0) | (d == nd - 1))
    def _():
        wait_bytes(rows_send, r_ssem)
        wait_bytes(q_send, qh_ssem)


def back_kernel(fwd, pivots, out, solution_x, out_sem):
    def result(b):
        rows = pl.ds(pl.multiple_of(b * RB, RB), RB)
        return pltpu.make_async_copy(solution_x.at[:, rows, :], out.at[:, rows, :], out_sem.at[b])

    steps = fwd.shape[1] // RB

    @pl.loop(0, steps)
    def _(b):
        rows = pl.ds(pl.multiple_of(b * RB, RB), RB)
        solved = fwd[NL - 1, rows, :]
        solution_x[NL - 1, rows, :] = solved
        for layer in range(NL - 2, -1, -1):
            solved = fwd[layer, rows, :] + pivots[layer, rows, :] * solved
            solution_x[layer, rows, :] = solved
        result(b).start()

    @pl.loop(0, steps)
    def _(b):
        result(b).wait()


def body(noise, kappa, mask):
    na, nd = lax.axis_size("ax"), lax.axis_size("ay")
    br = nd * SR
    ext = br + 2 * TOP
    dma = pltpu.SemaphoreType.DMA
    scratch = [
        pltpu.VMEM((NL, SR, nd * BC), F32),
        pltpu.VMEM((br, BC), jnp.int32),
        pltpu.VMEM((NL, ext, BC), F32),
        pltpu.VMEM((NL, ext, BC), F32),
        pltpu.VMEM((NL + 2, 2, ext, 128), F32),
        pltpu.VMEM((NL + 2, 2, ext, 128), F32),
        pltpu.VMEM((NL, ext, 128), F32),
        pltpu.VMEM((NL // 4, 8, nd * BC), F32),
        pltpu.VMEM((2, NL // 4, 8, BC), F32),
        pltpu.VMEM((2, NL // 4, 8, BC), F32),
        pltpu.VMEM((2, NL // 4, 8, BC), F32),
        pltpu.VMEM((nd, 8, 128), F32),
        pltpu.VMEM((nd + 2, 8, 128), F32),
        pltpu.VMEM((ext, 128), F32),
        pltpu.VMEM((ext, 128), F32),
        pltpu.VMEM((ext, 128), F32),
        pltpu.VMEM((ext, 128), F32),
        pltpu.VMEM((ext, 128), F32),
        pltpu.VMEM((br, 128), F32),
        pltpu.VMEM((2, br // 4, 128), F32),
        pltpu.VMEM((2, br // 4, 128), F32),
        pltpu.VMEM((2, 2, 8, 128), F32),
        dma((3,)), dma, dma((NL,)),
        dma, dma,
        dma, dma((2,)),
        dma, dma((2,)),
        dma((2,)), dma((2,)),
        dma((2,)), dma((2,)),
        dma((2, 2)), dma((2, 2)),
    ]
    field = pltpu.VMEM((NL, br, BC), F32)
    forward, pivots = pl.pallas_call(
        functools.partial(kernel, na, nd),
        out_shape=(field, field),
        in_specs=[pl.BlockSpec(memory_space=pltpu.HBM)] * 3,
        out_specs=[pl.BlockSpec(memory_space=pltpu.VMEM)] * 2,
        scratch_shapes=scratch,
        compiler_params=pltpu.CompilerParams(collective_id=0, has_side_effects=True, vmem_limit_bytes=48 << 20),
        name="sweeps",
    )(noise, kappa, mask)
    return pl.pallas_call(
        back_kernel,
        out_shape=jax.ShapeDtypeStruct((NL, br, BC), F32),
        in_specs=[pl.BlockSpec(memory_space=pltpu.VMEM)] * 2,
        out_specs=pl.BlockSpec(memory_space=pltpu.HBM),
        scratch_shapes=[field, dma((br // RB,))],
        compiler_params=pltpu.CompilerParams(vmem_limit_bytes=16 << 20),
        name="back",
    )(forward, pivots)


def solution(mesh):
    in_specs = (P(None, ("ax", "ay"), None), P(None, "ax", "ay"), P("ax", "ay"))
    out_specs = P(None, "ax", "ay")
    return jax.shard_map(body, mesh=mesh, in_specs=in_specs, out_specs=out_specs, check_vma=False)
```

```python
import functools

import jax
import jax.numpy as jnp
from jax import lax
from jax.experimental import pallas as pl
from jax.experimental.pallas import tpu as pltpu
from jax.sharding import PartitionSpec as P

MESH = pl.DeviceIdType.MESH
F32 = jnp.float32
NL = 16
SR = 16
BC = 256
TOP = 16
LAG = 2
RB = 32
COLS = (slice(0, 128), slice(128, 256))
EARLY = 4


def wait_bytes(ref, sem):
    pltpu.make_async_copy(ref, ref, sem).wait()


def around(field, layer, first, here, outer):
    rows = pl.ds(first, 8)
    lane = lax.broadcasted_iota(jnp.int32, (8, 128), 1)
    lane_l, lane_r = lane == 0, lane == 127
    back = [pltpu.roll(x, 1, 1) for x in here]
    fore = [pltpu.roll(x, 127, 1) for x in here]
    side = (
        jnp.where(lane_l, outer, back[0]) + jnp.where(lane_r, fore[1], fore[0]),
        jnp.where(lane_l, back[0], back[1]) + jnp.where(lane_r, outer, fore[1]),
    )
    return [
        side[c] + (field[layer + 1, c, pl.ds(first - 1, 8), :] + field[layer + 1, c, pl.ds(first + 1, 8), :])
        + field[layer, c, rows, :]
        for c in range(2)
    ]

def group(refs, step, first, do_initial, do_middle, do_smooth):
    fwd, kap, noise_x, inv_x, init_x, mid_x, mid_h, h_init, h_mid, h_inv = refs
    rows = pl.ds(first, 8)
    lane = lax.broadcasted_iota(jnp.int32, (8, 128), 1)
    stores = []
    initial = middle = None
    if do_initial:
        initial = [inv_x[step, rows, COLS[c]] * noise_x[step, rows, COLS[c]] for c in range(2)]
        stores += [(init_x, (step + 1, c, rows, slice(None)), initial[c]) for c in range(2)]
    if do_middle:
        layer = step - 1
        turn = lax.rem(254 - 4 * layer, 128)
        here = [init_x[layer + 1, c, rows, :] for c in range(2)]
        total = around(init_x, layer, first, here, pltpu.roll(h_init[rows, :], turn, 1))
        if initial is not None:
            total = [total[c] + initial[c] for c in range(2)]
        middle = [inv_x[layer, rows, COLS[c]] * (noise_x[layer, rows, COLS[c]] + total[c]) for c in range(2)]
        inner = jnp.where(lane < 64, here[0], here[1])
        outer = pltpu.roll(h_mid[rows, :], turn, 1) + pltpu.roll(h_inv[rows, :], turn, 1) * inner
        stores += [(mid_x, (layer + 1, c, rows, slice(None)), middle[c]) for c in range(2)]
        stores += [(mid_h, (layer, rows, slice(None)), outer)]
    if do_smooth:
        layer = step - 2
        own = pl.ds(pl.multiple_of(first - TOP, 8), 8)
        here = [mid_x[layer + 1, c, rows, :] for c in range(2)]
        total = around(mid_x, layer, first, here, mid_h[layer, rows, :])
        if middle is not None:
            total = [total[c] + middle[c] for c in range(2)]
        for c in range(2):
            field = inv_x[layer, rows, COLS[c]] * (noise_x[layer, rows, COLS[c]] + total[c])
            previous = fwd[lax.max(layer - 1, 0), own, COLS[c]]
            pivot = kap[layer, own, COLS[c]]
            stores += [(fwd, (layer, own, COLS[c]), (field + previous) * pivot)]
    return stores


def put(stores):
    for ref, index, value in stores:
        ref[index] = value


def kernel(na, nd, noise, kappa, mask, *refs):
    fwd, kap, noise_x, inv_x, init_x, mid_x, mid_h, h_init, h_mid, h_inv = refs[:10]
    (strip, msk, rows_send, rowi_send, rown, rowi, q_send, q_recv, qn, qp, e_send, f_send, f_recv, c_recv, load_sem, bulk_send, bulk_recv, q_ssem, q_rsem, r_ssem, r_rsem, qh_ssem, qh_rsem,
     e_ssem, e_rsem, i_ssem, i_rsem, c_ssem, c_rsem) = refs[10:]
    br = nd * SR
    end = TOP + br
    a, d = lax.axis_index("ax"), lax.axis_index("ay")
    above, below = lax.rem(a + na - 1, na), lax.rem(a + 1, na)
    left, right = lax.rem(d + nd - 1, nd), lax.rem(d + 1, nd)

    loads = [
        pltpu.make_async_copy(noise, strip, load_sem.at[0]),
        pltpu.make_async_copy(kappa, kap, load_sem.at[1]),
        pltpu.make_async_copy(mask, msk, load_sem.at[2]),
    ]
    for load in loads:
        load.start()

    barrier = pltpu.get_barrier_semaphore()

    def greet(x, y):
        pl.semaphore_signal(barrier, inc=1, device_id=(x, y), device_id_type=MESH)

    @pl.loop(1, nd)
    def _(k):
        greet(a, lax.rem(d + k, nd))

    edge = jnp.where(d == 0, nd, 0) + jnp.where(d == nd - 1, nd, 0)
    odd = lax.rem(a, 2)

    @pl.when(odd == 0)
    def _():
        @pl.loop(0, nd)
        def _(k):
            greet(above, lax.rem(d + k, nd))
            greet(below, lax.rem(d + k, nd))

    pl.semaphore_wait(barrier, nd - 1 + odd * (2 * nd))

    @pl.when(odd == 1)
    def _():
        for x in (above, below):
            for y in (d, left, right):
                greet(x, y)
        greet(above, nd - 1)
        greet(below, 0)
        for y, x in ((0, above), (nd - 1, below)):
            @pl.when(d == y)
            def _():
                @pl.loop(0, nd)
                def _(t):
                    greet(x, t)

    def bulk(layer):
        pltpu.make_async_copy(
            noise.at[layer, :, pl.ds(pl.multiple_of(d * BC, BC), BC)],
            noise_x.at[layer, pl.ds(pl.multiple_of(TOP + d * SR, SR), SR), :],
            bulk_recv.at[layer],
        ).start()

        @pl.loop(1, nd)
        def _(k):
            t = lax.rem(d + k, nd)
            pltpu.make_async_remote_copy(
                src_ref=noise.at[layer, :, pl.ds(pl.multiple_of(t * BC, BC), BC)],
                dst_ref=noise_x.at[layer, pl.ds(pl.multiple_of(TOP + d * SR, SR), SR), :],
                send_sem=bulk_send,
                recv_sem=bulk_recv.at[layer],
                device_id=(a, t),
                device_id_type=MESH,
            ).start()

    @pl.loop(0, EARLY)
    def _(layer):
        bulk(layer)

    lane = lax.broadcasted_iota(jnp.int32, (8, 128), 1)
    sub = lax.broadcasted_iota(jnp.int32, (8, BC), 0)

    loads[0].wait()

    @pl.loop(0, nd)
    def _(t):
        before = pl.multiple_of(lax.rem(t + nd - 1, nd) * BC + 128, 128)
        after = pl.multiple_of(lax.rem(t + 1, nd) * BC, 128)
        packed = jnp.zeros((8, 128), F32)
        for layer in range(NL):
            for half in range(2):
                rows = slice(half * 8, half * 8 + 8)
                both = jnp.where(lane < 64, strip[layer, rows, pl.ds(after, 128)], strip[layer, rows, pl.ds(before, 128)])
                packed = jnp.where(lane // 4 == layer + 16 * half, pltpu.roll(both, (4 * layer + 2 + 64 * half) % 128, 1), packed)
        q_send[t] = packed

    def q_place(s):
        return q_recv.at[s + 1]

    pltpu.make_async_copy(q_send.at[d], q_place(d), q_rsem).start()

    @pl.loop(1, nd)
    def _(k):
        t = lax.rem(d + k, nd)
        pltpu.make_async_remote_copy(
            src_ref=q_send.at[t], dst_ref=q_place(d), send_sem=q_ssem, recv_sem=q_rsem,
            device_id=(a, t), device_id_type=MESH,
        ).start()

    def pick_rows(tile, first, i):
        return pltpu.roll(tile, (2 * i - first) % 8, 0)

    def send_rows(first_row, first, x, slot):
        @pl.loop(0, nd)
        def _(t):
            cols = pl.ds(pl.multiple_of(t * BC, BC), BC)
            for q in range(NL // 4):
                packed = jnp.zeros((8, BC), F32)
                for i in range(4):
                    tile = strip[4 * q + i, first_row:first_row + 8, cols]
                    packed = jnp.where(sub // 2 == i, pick_rows(tile, first, i), packed)
                rows_send[q, :, cols] = packed
            pltpu.make_async_remote_copy(
                src_ref=rows_send.at[:, :, cols], dst_ref=rown.at[slot], send_sem=r_ssem, recv_sem=r_rsem.at[slot],
                device_id=(x, t), device_id_type=MESH,
            ).start()
            pltpu.make_async_remote_copy(
                src_ref=q_send.at[t], dst_ref=q_recv.at[(0, nd + 1)[slot]], send_sem=qh_ssem,
                recv_sem=qh_rsem.at[slot], device_id=(x, t), device_id_type=MESH,
            ).start()

    @pl.when(odd == 0)
    def _():
        pl.semaphore_wait(barrier, 8 + edge)

    @pl.when(d == 0)
    def _():
        send_rows(0, 0, above, 1)

    @pl.when(d == nd - 1)
    def _():
        send_rows(SR - 8, 6, below, 0)

    loads[1].wait()
    loads[2].wait()
    rb = 32
    lane_b = lax.broadcasted_iota(jnp.int32, (rb, 128), 1)

    @pl.loop(0, br // rb)
    def _(b):
        rows = pl.ds(pl.multiple_of(b * rb, rb), rb)
        active = msk[rows, :].astype(F32)
        packed = jnp.zeros((rb, 128), F32)
        for layer in range(NL):
            inverse = active / (6.0 + kap[layer, rows, :])
            inv_x[layer, pl.ds(pl.multiple_of(TOP + b * rb, 16), rb), :] = inverse
            both = jnp.where(lane_b < 64, inverse[:, :128], inverse[:, 128:])
            packed = jnp.where(lane_b // 4 == layer, pltpu.roll(both, (4 * layer + 2) % 128, 1), packed)
        e_send[rows, :] = packed

    folds = ((0, 2, 64, 66), (0, 126, 64, 62))
    fr = br // 4
    place = lane % 4

    @pl.loop(0, fr // 8)
    def _(b):
        for slot in range(2):
            packed = jnp.zeros((8, 128), F32)
            for k in range(4):
                piece = pltpu.roll(e_send[pl.ds(pl.multiple_of(k * fr + b * 8, 8), 8), :], folds[slot][k], 1)
                low = (0, 2, 0, 2)[k] if slot == 0 else (2, 0, 2, 0)[k]
                mine = (place >= low) & (place < low + 2) & (lane // 64 == k // 2)
                packed = jnp.where(mine, piece, packed)
            f_send[slot, pl.ds(pl.multiple_of(b * 8, 8), 8), :] = packed

    halos = []
    for slot, y in ((0, right), (1, left)):
        halos.append(pltpu.make_async_remote_copy(
            src_ref=f_send.at[slot], dst_ref=f_recv.at[slot], send_sem=e_ssem.at[slot], recv_sem=e_rsem.at[slot],
            device_id=(a, y), device_id_type=MESH,
        ))
        halos.append(pltpu.make_async_remote_copy(
            src_ref=e_send.at[br - 8:br, :], dst_ref=c_recv.at[slot, 0], send_sem=c_ssem.at[slot, 0],
            recv_sem=c_rsem.at[slot, 0], device_id=(below, y), device_id_type=MESH,
        ))
        halos.append(pltpu.make_async_remote_copy(
            src_ref=e_send.at[0:8, :], dst_ref=c_recv.at[slot, 1], send_sem=c_ssem.at[slot, 1],
            recv_sem=c_rsem.at[slot, 1], device_id=(above, y), device_id_type=MESH,
        ))
    for q in range(NL // 4):
        down = jnp.zeros((8, BC), F32)
        up = jnp.zeros((8, BC), F32)
        for i in range(4):
            layer = 4 * q + i
            down = jnp.where(sub // 2 == i, pick_rows(inv_x[layer, end - 8:end, :], 6, i), down)
            up = jnp.where(sub // 2 == i, pick_rows(inv_x[layer, TOP:TOP + 8, :], 0, i), up)
        rowi_send[0, q] = down
        rowi_send[1, q] = up
    for slot, x in ((0, below), (1, above)):
        halos.append(pltpu.make_async_remote_copy(
            src_ref=rowi_send.at[slot], dst_ref=rowi.at[slot], send_sem=i_ssem.at[slot], recv_sem=i_rsem.at[slot],
            device_id=(x, d), device_id_type=MESH,
        ))
    for halo in halos:
        halo.start()

    @pl.loop(EARLY, NL)
    def _(layer):
        bulk(layer)

    @pl.loop(0, br // rb)
    def _(b):
        rows = pl.ds(pl.multiple_of(b * rb, rb), rb)
        pivot = jnp.zeros((rb, BC), F32)
        for layer in range(NL):
            pivot = 1.0 / (2.5 + kap[layer, rows, :] - pivot)
            kap[layer, rows, :] = pivot

    @pl.loop(0, (br + 16) // 16)
    def _(b):
        rows = pl.ds(pl.multiple_of(8 + b * 16, 8), 16)
        for field in (init_x, mid_x):
            for layer in (0, NL + 1):
                for c in range(2):
                    field[layer, c, rows, :] = jnp.zeros((16, 128), F32)

    for halo in halos:
        halo.wait()
    for slot in range(2):
        wait_bytes(rown.at[slot], r_rsem.at[slot])
        wait_bytes(q_recv.at[slot], qh_rsem.at[slot])
    wait_bytes(q_recv.at[1:nd + 1], q_rsem)
    keep_top = jnp.where(a > 0, 1.0, 0.0).astype(F32)
    keep_end = jnp.where(a < na - 1, 1.0, 0.0).astype(F32)
    keep_left = jnp.where(d > 0, 1.0, 0.0).astype(F32)
    keep_right = jnp.where(d < nd - 1, 1.0, 0.0).astype(F32)

    @pl.loop(0, NL // 4)
    def _(q):
        for i in range(4):
            layer = 4 * q + i
            inv_x[layer, TOP - 8:TOP, :] = keep_top * pltpu.roll(rowi[0, q], (6 - 2 * i) % 8, 0)
            inv_x[layer, end:end + 8, :] = keep_end * pltpu.roll(rowi[1, q], (-2 * i) % 8, 0)
            noise_x[layer, TOP - 8:TOP, :] = pltpu.roll(rown[0, q], (6 - 2 * i) % 8, 0)
            noise_x[layer, end:end + 8, :] = pltpu.roll(rown[1, q], (-2 * i) % 8, 0)

    groups = (br + 16) // 8

    def beside(packed):
        return jnp.where(place == 1, pltpu.roll(packed, 127, 1), pltpu.roll(packed, 1, 1))

    def sides(first, from_left, from_right, noise_q):
        rows = pl.ds(first, 8)
        inverse = jnp.where(place < 2, from_left * keep_left, from_right * keep_right)
        qn[rows, :] = noise_q
        qp[rows, :] = inverse * noise_q
        h_inv[rows, :] = inverse

    sides(TOP - 8, c_recv[0, 0] * keep_top, c_recv[1, 0] * keep_top, pltpu.roll(q_recv[0], 64, 1))
    sides(end, c_recv[0, 1] * keep_end, c_recv[1, 1] * keep_end, q_recv[nd + 1])
    for k in range(4):
        @pl.loop(0, fr // SR)
        def _(b):
            noise_q = q_recv[1 + k * (fr // SR) + b]
            for half in range(2):
                rows = pl.ds(pl.multiple_of(b * SR + half * 8, 8), 8)
                pieces = [pltpu.roll(f_recv[slot, rows, :], (128 - folds[slot][k]) % 128, 1) for slot in range(2)]
                first = pl.multiple_of(TOP + k * fr + b * SR + half * 8, 8)
                sides(first, *pieces, pltpu.roll(noise_q, 64, 1) if half else noise_q)

    @pl.loop(0, br // 8)
    def _(b):
        first = pl.multiple_of(TOP + b * 8, 8)
        rows = pl.ds(first, 8)
        here = qp[rows, :]
        total = qp[pl.ds(first - 1, 8), :] + qp[pl.ds(first + 1, 8), :]
        total = total + jnp.where(place < 2, pltpu.roll(here, 1, 1), pltpu.roll(here, 127, 1))
        total = total + jnp.where(lane < 4, 0.0, pltpu.roll(here, 4, 1))
        total = total + jnp.where(lane >= 60, 0.0, pltpu.roll(here, 124, 1))
        inverse = h_inv[rows, :]
        h_mid[rows, :] = beside(inverse * (qn[rows, :] + total))
        h_inv[rows, :] = beside(inverse)

    @pl.loop(0, groups)
    def _(b):
        rows = pl.ds(pl.multiple_of(8 + b * 8, 8), 8)
        h_init[rows, :] = beside(qp[rows, :])

    @pl.loop(0, br // 8)
    def _(b):
        fwd[0, pl.ds(pl.multiple_of(b * 8, 8), 8), :] = jnp.zeros((8, BC), F32)

    def sweep(step, do_initial, do_middle, do_smooth):
        pending = []
        low, high = (0, groups) if do_middle else (1, groups - 1)
        for g in range(low, high):
            pending.append(group(refs[:10], step, 8 + 8 * g, do_initial, do_middle, do_smooth and 1 <= g < groups - 1))
            if len(pending) > LAG:
                put(pending.pop(0))
        for stores in pending:
            put(stores)

    for step in range(2):
        wait_bytes(noise_x.at[step, TOP:end, :], bulk_recv.at[step])

        @pl.loop(0, groups)
        def _(b):
            put(group(refs[:10], step, pl.multiple_of(8 + b * 8, 8), True, step > 0, False))

    @pl.loop(2, NL - 1)
    def _(step):
        wait_bytes(noise_x.at[step, TOP:end, :], bulk_recv.at[step])
        sweep(step, True, True, True)

    wait_bytes(noise_x.at[NL - 1, TOP:end, :], bulk_recv.at[NL - 1])

    wait_bytes(noise.at[:, :, :(nd - 1) * BC], bulk_send)

    wait_bytes(q_send.at[:nd - 1], q_ssem)

    @pl.when((d == 0) | (d == nd - 1))
    def _():
        wait_bytes(rows_send, r_ssem)
        wait_bytes(q_send, qh_ssem)


def back_kernel(*refs):
    fwd, kap = refs[:2]
    out, solution_x, out_sem = refs[10:]
    size = RB // 8
    steps = fwd.shape[1] // RB

    def result(b):
        rows = pl.ds(b * RB, RB)
        return pltpu.make_async_copy(solution_x.at[:, rows, :], out.at[:, rows, :], out_sem.at[b])

    def sweep_group(step, g, do_initial, do_middle):
        inside = 0 < g < last
        if not 0 <= g <= last or not (inside or do_middle):
            return []
        return group(refs[:10], step, 8 + 8 * g, do_initial, do_middle, inside)

    def back(g):
        rows = pl.ds(8 * g - 8, 8)
        for c in COLS:
            solved = fwd[NL - 1, rows, c]
            solution_x[NL - 1, rows, c] = solved
            for layer in range(NL - 2, -1, -1):
                solved = fwd[layer, rows, c] + kap[layer, rows, c] * solved
                solution_x[layer, rows, c] = solved

    last = steps * size + 1
    pending = []
    for turn in range(last + 10):
        pending.append([])
        if len(pending) > LAG:
            put(pending.pop(0))
        for lag, stage in ((0, (NL - 1, True, True)), (3, (NL, False, True)), (6, (NL + 1, False, False))):
            pending[-1] += sweep_group(stage[0], turn - lag, *stage[1:])
        g = turn - 9
        if 0 < g < last:
            back(g)
            if g % size == 0:
                result(g // size - 1).start()

    for b in range(steps):
        result(b).wait()


def body(noise, kappa, mask):
    na, nd = lax.axis_size("ax"), lax.axis_size("ay")
    br = nd * SR
    ext = br + 2 * TOP
    dma = pltpu.SemaphoreType.DMA
    scratch = [
        pltpu.VMEM((NL, SR, nd * BC), F32),
        pltpu.VMEM((br, BC), jnp.int32),
        pltpu.VMEM((NL // 4, 8, nd * BC), F32),
        pltpu.VMEM((2, NL // 4, 8, BC), F32),
        pltpu.VMEM((2, NL // 4, 8, BC), F32),
        pltpu.VMEM((2, NL // 4, 8, BC), F32),
        pltpu.VMEM((nd, 8, 128), F32),
        pltpu.VMEM((nd + 2, 8, 128), F32),
        pltpu.VMEM((ext, 128), F32),
        pltpu.VMEM((ext, 128), F32),
        pltpu.VMEM((br, 128), F32),
        pltpu.VMEM((2, br // 4, 128), F32),
        pltpu.VMEM((2, br // 4, 128), F32),
        pltpu.VMEM((2, 2, 8, 128), F32),
        dma((3,)), dma, dma((NL,)),
        dma, dma,
        dma, dma((2,)),
        dma, dma((2,)),
        dma((2,)), dma((2,)),
        dma((2,)), dma((2,)),
        dma((2, 2)), dma((2, 2)),
    ]
    field = pltpu.VMEM((NL, br, BC), F32)
    fields = (
        field, field,
        pltpu.VMEM((NL, ext, BC), F32),
        pltpu.VMEM((NL, ext, BC), F32),
        pltpu.VMEM((NL + 2, 2, ext, 128), F32),
        pltpu.VMEM((NL + 2, 2, ext, 128), F32),
        pltpu.VMEM((NL, ext, 128), F32),
        pltpu.VMEM((ext, 128), F32),
        pltpu.VMEM((ext, 128), F32),
        pltpu.VMEM((ext, 128), F32),
    )
    fields = pl.pallas_call(
        functools.partial(kernel, na, nd),
        out_shape=fields,
        in_specs=[pl.BlockSpec(memory_space=pltpu.HBM)] * 3,
        out_specs=[pl.BlockSpec(memory_space=pltpu.VMEM)] * 10,
        scratch_shapes=scratch,
        compiler_params=pltpu.CompilerParams(collective_id=0, has_side_effects=True, vmem_limit_bytes=16 << 20),
        name="sweeps",
    )(*(pltpu.with_memory_space_constraint(x, pltpu.HBM) for x in (noise, kappa, mask)))
    return pl.pallas_call(
        back_kernel,
        out_shape=jax.ShapeDtypeStruct((NL, br, BC), F32),
        in_specs=[pl.BlockSpec(memory_space=pltpu.VMEM)] * 10,
        out_specs=pl.BlockSpec(memory_space=pltpu.HBM),
        scratch_shapes=[field, dma((br // RB,))],
        compiler_params=pltpu.CompilerParams(vmem_limit_bytes=16 << 20),
        name="back",
    )(*fields)


def solution(mesh):
    in_specs = (P(None, ("ax", "ay"), None), P(None, "ax", "ay"), P("ax", "ay"))
    out_specs = P(None, "ax", "ay")
    return jax.shard_map(body, mesh=mesh, in_specs=in_specs, out_specs=out_specs, check_vma=False)
```

```python
import functools

import jax
import jax.numpy as jnp
from jax import lax
from jax.experimental import pallas as pl
from jax.experimental.pallas import tpu as pltpu
from jax.sharding import PartitionSpec as P

MESH = pl.DeviceIdType.MESH
F32 = jnp.float32
NL = 16
SR = 16
BC = 256
TOP = 16
LAG = 2
WB = 16
COLS = (slice(0, 128), slice(128, 256))
EARLY = 4


def wait_bytes(ref, sem):
    pltpu.make_async_copy(ref, ref, sem).wait()


def around(field, layer, first, here, outer):
    rows = pl.ds(first, 8)
    lane = lax.broadcasted_iota(jnp.int32, (8, 128), 1)
    lane_l, lane_r = lane == 0, lane == 127
    back = [pltpu.roll(x, 1, 1) for x in here]
    fore = [pltpu.roll(x, 127, 1) for x in here]
    side = (
        jnp.where(lane_l, outer, back[0]) + jnp.where(lane_r, fore[1], fore[0]),
        jnp.where(lane_l, back[0], back[1]) + jnp.where(lane_r, outer, fore[1]),
    )
    return [
        side[c] + (field[layer + 1, c, pl.ds(first - 1, 8), :] + field[layer + 1, c, pl.ds(first + 1, 8), :])
        + field[layer, c, rows, :]
        for c in range(2)
    ]

def group(refs, step, first, do_initial, do_middle, do_smooth):
    fwd, kap, noise_x, inv_x, init_x, mid_x, mid_h, h_init, h_mid, h_inv = refs
    rows = pl.ds(first, 8)
    lane = lax.broadcasted_iota(jnp.int32, (8, 128), 1)
    stores = []
    initial = middle = None
    if do_initial:
        initial = [inv_x[step, rows, COLS[c]] * noise_x[step, rows, COLS[c]] for c in range(2)]
        stores += [(init_x, (step + 1, c, rows, slice(None)), initial[c]) for c in range(2)]
    if do_middle:
        layer = step - 1
        turn = lax.rem(254 - 4 * layer, 128)
        here = [init_x[layer + 1, c, rows, :] for c in range(2)]
        total = around(init_x, layer, first, here, pltpu.roll(h_init[rows, :], turn, 1))
        if initial is not None:
            total = [total[c] + initial[c] for c in range(2)]
        middle = [inv_x[layer, rows, COLS[c]] * (noise_x[layer, rows, COLS[c]] + total[c]) for c in range(2)]
        inner = jnp.where(lane < 64, here[0], here[1])
        outer = pltpu.roll(h_mid[rows, :], turn, 1) + pltpu.roll(h_inv[rows, :], turn, 1) * inner
        stores += [(mid_x, (layer + 1, c, rows, slice(None)), middle[c]) for c in range(2)]
        stores += [(mid_h, (layer, rows, slice(None)), outer)]
    if do_smooth:
        layer = step - 2
        own = pl.ds(pl.multiple_of(first - TOP, 8), 8)
        here = [mid_x[layer + 1, c, rows, :] for c in range(2)]
        total = around(mid_x, layer, first, here, mid_h[layer, rows, :])
        if middle is not None:
            total = [total[c] + middle[c] for c in range(2)]
        for c in range(2):
            field = inv_x[layer, rows, COLS[c]] * (noise_x[layer, rows, COLS[c]] + total[c])
            previous = fwd[lax.max(layer - 1, 0), own, COLS[c]]
            pivot = kap[layer, own, COLS[c]]
            stores += [(fwd, (layer, own, COLS[c]), (field + previous) * pivot)]
    return stores


def put(stores):
    for ref, index, value in stores:
        ref[index] = value


def kernel(na, nd, noise, kappa, mask, *refs):
    fwd, kap, noise_x, inv_x, init_x, mid_x, mid_h, h_init, h_mid, h_inv = refs[:10]
    (strip, msk, rows_send, rowi_send, rown, rowi, q_send, q_recv, qn, qp, e_send, f_send, f_recv, c_recv, load_sem, bulk_send, bulk_recv, q_ssem, q_rsem, r_ssem, r_rsem, qh_ssem, qh_rsem,
     e_ssem, e_rsem, i_ssem, i_rsem, c_ssem, c_rsem) = refs[10:]
    br = nd * SR
    end = TOP + br
    a, d = lax.axis_index("ax"), lax.axis_index("ay")
    above, below = lax.rem(a + na - 1, na), lax.rem(a + 1, na)
    left, right = lax.rem(d + nd - 1, nd), lax.rem(d + 1, nd)

    loads = [
        pltpu.make_async_copy(noise, strip, load_sem.at[0]),
        pltpu.make_async_copy(kappa, kap, load_sem.at[1]),
        pltpu.make_async_copy(mask, msk, load_sem.at[2]),
    ]
    for load in loads:
        load.start()

    barrier = pltpu.get_barrier_semaphore()

    def greet(x, y):
        pl.semaphore_signal(barrier, inc=1, device_id=(x, y), device_id_type=MESH)

    @pl.loop(1, nd)
    def _(k):
        greet(a, lax.rem(d + k, nd))

    edge = jnp.where(d == 0, nd, 0) + jnp.where(d == nd - 1, nd, 0)
    odd = lax.rem(a, 2)

    @pl.when(odd == 0)
    def _():
        @pl.loop(0, nd)
        def _(k):
            greet(above, lax.rem(d + k, nd))
            greet(below, lax.rem(d + k, nd))

    pl.semaphore_wait(barrier, nd - 1 + odd * (2 * nd))

    @pl.when(odd == 1)
    def _():
        for x in (above, below):
            for y in (d, left, right):
                greet(x, y)
        greet(above, nd - 1)
        greet(below, 0)
        for y, x in ((0, above), (nd - 1, below)):
            @pl.when(d == y)
            def _():
                @pl.loop(0, nd)
                def _(t):
                    greet(x, t)

    def bulk(layer):
        pltpu.make_async_copy(
            noise.at[layer, :, pl.ds(pl.multiple_of(d * BC, BC), BC)],
            noise_x.at[layer, pl.ds(pl.multiple_of(TOP + d * SR, SR), SR), :],
            bulk_recv.at[layer],
        ).start()

        @pl.loop(1, nd)
        def _(k):
            t = lax.rem(d + k, nd)
            pltpu.make_async_remote_copy(
                src_ref=noise.at[layer, :, pl.ds(pl.multiple_of(t * BC, BC), BC)],
                dst_ref=noise_x.at[layer, pl.ds(pl.multiple_of(TOP + d * SR, SR), SR), :],
                send_sem=bulk_send,
                recv_sem=bulk_recv.at[layer],
                device_id=(a, t),
                device_id_type=MESH,
            ).start()

    @pl.loop(0, EARLY)
    def _(layer):
        bulk(layer)

    lane = lax.broadcasted_iota(jnp.int32, (8, 128), 1)
    sub = lax.broadcasted_iota(jnp.int32, (8, BC), 0)

    loads[0].wait()

    @pl.loop(0, nd)
    def _(t):
        before = pl.multiple_of(lax.rem(t + nd - 1, nd) * BC + 128, 128)
        after = pl.multiple_of(lax.rem(t + 1, nd) * BC, 128)
        packed = jnp.zeros((8, 128), F32)
        for layer in range(NL):
            for half in range(2):
                rows = slice(half * 8, half * 8 + 8)
                both = jnp.where(lane < 64, strip[layer, rows, pl.ds(after, 128)], strip[layer, rows, pl.ds(before, 128)])
                packed = jnp.where(lane // 4 == layer + 16 * half, pltpu.roll(both, (4 * layer + 2 + 64 * half) % 128, 1), packed)
        q_send[t] = packed

    def q_place(s):
        return q_recv.at[s + 1]

    pltpu.make_async_copy(q_send.at[d], q_place(d), q_rsem).start()

    @pl.loop(1, nd)
    def _(k):
        t = lax.rem(d + k, nd)
        pltpu.make_async_remote_copy(
            src_ref=q_send.at[t], dst_ref=q_place(d), send_sem=q_ssem, recv_sem=q_rsem,
            device_id=(a, t), device_id_type=MESH,
        ).start()

    def pick_rows(tile, first, i):
        return pltpu.roll(tile, (2 * i - first) % 8, 0)

    def send_rows(first_row, first, x, slot):
        @pl.loop(0, nd)
        def _(t):
            cols = pl.ds(pl.multiple_of(t * BC, BC), BC)
            for q in range(NL // 4):
                packed = jnp.zeros((8, BC), F32)
                for i in range(4):
                    tile = strip[4 * q + i, first_row:first_row + 8, cols]
                    packed = jnp.where(sub // 2 == i, pick_rows(tile, first, i), packed)
                rows_send[q, :, cols] = packed
            pltpu.make_async_remote_copy(
                src_ref=rows_send.at[:, :, cols], dst_ref=rown.at[slot], send_sem=r_ssem, recv_sem=r_rsem.at[slot],
                device_id=(x, t), device_id_type=MESH,
            ).start()
            pltpu.make_async_remote_copy(
                src_ref=q_send.at[t], dst_ref=q_recv.at[(0, nd + 1)[slot]], send_sem=qh_ssem,
                recv_sem=qh_rsem.at[slot], device_id=(x, t), device_id_type=MESH,
            ).start()

    @pl.when(odd == 0)
    def _():
        pl.semaphore_wait(barrier, 8 + edge)

    @pl.when(d == 0)
    def _():
        send_rows(0, 0, above, 1)

    @pl.when(d == nd - 1)
    def _():
        send_rows(SR - 8, 6, below, 0)

    loads[1].wait()
    loads[2].wait()
    rb = 32
    lane_b = lax.broadcasted_iota(jnp.int32, (rb, 128), 1)

    @pl.loop(0, br // rb)
    def _(b):
        rows = pl.ds(pl.multiple_of(b * rb, rb), rb)
        active = msk[rows, :].astype(F32)
        packed = jnp.zeros((rb, 128), F32)
        for layer in range(NL):
            inverse = active / (6.0 + kap[layer, rows, :])
            inv_x[layer, pl.ds(pl.multiple_of(TOP + b * rb, 16), rb), :] = inverse
            both = jnp.where(lane_b < 64, inverse[:, :128], inverse[:, 128:])
            packed = jnp.where(lane_b // 4 == layer, pltpu.roll(both, (4 * layer + 2) % 128, 1), packed)
        e_send[rows, :] = packed

    folds = ((0, 2, 64, 66), (0, 126, 64, 62))
    fr = br // 4
    place = lane % 4

    @pl.loop(0, fr // 8)
    def _(b):
        for slot in range(2):
            packed = jnp.zeros((8, 128), F32)
            for k in range(4):
                piece = pltpu.roll(e_send[pl.ds(pl.multiple_of(k * fr + b * 8, 8), 8), :], folds[slot][k], 1)
                low = (0, 2, 0, 2)[k] if slot == 0 else (2, 0, 2, 0)[k]
                mine = (place >= low) & (place < low + 2) & (lane // 64 == k // 2)
                packed = jnp.where(mine, piece, packed)
            f_send[slot, pl.ds(pl.multiple_of(b * 8, 8), 8), :] = packed

    halos = []
    for slot, y in ((0, right), (1, left)):
        halos.append(pltpu.make_async_remote_copy(
            src_ref=f_send.at[slot], dst_ref=f_recv.at[slot], send_sem=e_ssem.at[slot], recv_sem=e_rsem.at[slot],
            device_id=(a, y), device_id_type=MESH,
        ))
        halos.append(pltpu.make_async_remote_copy(
            src_ref=e_send.at[br - 8:br, :], dst_ref=c_recv.at[slot, 0], send_sem=c_ssem.at[slot, 0],
            recv_sem=c_rsem.at[slot, 0], device_id=(below, y), device_id_type=MESH,
        ))
        halos.append(pltpu.make_async_remote_copy(
            src_ref=e_send.at[0:8, :], dst_ref=c_recv.at[slot, 1], send_sem=c_ssem.at[slot, 1],
            recv_sem=c_rsem.at[slot, 1], device_id=(above, y), device_id_type=MESH,
        ))
    for q in range(NL // 4):
        down = jnp.zeros((8, BC), F32)
        up = jnp.zeros((8, BC), F32)
        for i in range(4):
            layer = 4 * q + i
            down = jnp.where(sub // 2 == i, pick_rows(inv_x[layer, end - 8:end, :], 6, i), down)
            up = jnp.where(sub // 2 == i, pick_rows(inv_x[layer, TOP:TOP + 8, :], 0, i), up)
        rowi_send[0, q] = down
        rowi_send[1, q] = up
    for slot, x in ((0, below), (1, above)):
        halos.append(pltpu.make_async_remote_copy(
            src_ref=rowi_send.at[slot], dst_ref=rowi.at[slot], send_sem=i_ssem.at[slot], recv_sem=i_rsem.at[slot],
            device_id=(x, d), device_id_type=MESH,
        ))
    for halo in halos:
        halo.start()

    @pl.loop(EARLY, NL)
    def _(layer):
        bulk(layer)

    @pl.loop(0, br // rb)
    def _(b):
        rows = pl.ds(pl.multiple_of(b * rb, rb), rb)
        pivot = jnp.zeros((rb, BC), F32)
        for layer in range(NL):
            pivot = 1.0 / (2.5 + kap[layer, rows, :] - pivot)
            kap[layer, rows, :] = pivot

    @pl.loop(0, (br + 16) // 16)
    def _(b):
        rows = pl.ds(pl.multiple_of(8 + b * 16, 8), 16)
        for field in (init_x, mid_x):
            for layer in (0, NL + 1):
                for c in range(2):
                    field[layer, c, rows, :] = jnp.zeros((16, 128), F32)

    for halo in halos:
        halo.wait()
    for slot in range(2):
        wait_bytes(rown.at[slot], r_rsem.at[slot])
        wait_bytes(q_recv.at[slot], qh_rsem.at[slot])
    wait_bytes(q_recv.at[1:nd + 1], q_rsem)
    keep_top = jnp.where(a > 0, 1.0, 0.0).astype(F32)
    keep_end = jnp.where(a < na - 1, 1.0, 0.0).astype(F32)
    keep_left = jnp.where(d > 0, 1.0, 0.0).astype(F32)
    keep_right = jnp.where(d < nd - 1, 1.0, 0.0).astype(F32)

    @pl.loop(0, NL // 4)
    def _(q):
        for i in range(4):
            layer = 4 * q + i
            inv_x[layer, TOP - 8:TOP, :] = keep_top * pltpu.roll(rowi[0, q], (6 - 2 * i) % 8, 0)
            inv_x[layer, end:end + 8, :] = keep_end * pltpu.roll(rowi[1, q], (-2 * i) % 8, 0)
            noise_x[layer, TOP - 8:TOP, :] = pltpu.roll(rown[0, q], (6 - 2 * i) % 8, 0)
            noise_x[layer, end:end + 8, :] = pltpu.roll(rown[1, q], (-2 * i) % 8, 0)

    groups = (br + 16) // 8

    def beside(packed):
        return jnp.where(place == 1, pltpu.roll(packed, 127, 1), pltpu.roll(packed, 1, 1))

    def sides(first, from_left, from_right, noise_q):
        rows = pl.ds(first, 8)
        inverse = jnp.where(place < 2, from_left * keep_left, from_right * keep_right)
        qn[rows, :] = noise_q
        qp[rows, :] = inverse * noise_q
        h_inv[rows, :] = inverse

    sides(TOP - 8, c_recv[0, 0] * keep_top, c_recv[1, 0] * keep_top, pltpu.roll(q_recv[0], 64, 1))
    sides(end, c_recv[0, 1] * keep_end, c_recv[1, 1] * keep_end, q_recv[nd + 1])
    for k in range(4):
        @pl.loop(0, fr // SR)
        def _(b):
            noise_q = q_recv[1 + k * (fr // SR) + b]
            for half in range(2):
                rows = pl.ds(pl.multiple_of(b * SR + half * 8, 8), 8)
                pieces = [pltpu.roll(f_recv[slot, rows, :], (128 - folds[slot][k]) % 128, 1) for slot in range(2)]
                first = pl.multiple_of(TOP + k * fr + b * SR + half * 8, 8)
                sides(first, *pieces, pltpu.roll(noise_q, 64, 1) if half else noise_q)

    @pl.loop(0, br // 8)
    def _(b):
        first = pl.multiple_of(TOP + b * 8, 8)
        rows = pl.ds(first, 8)
        here = qp[rows, :]
        total = qp[pl.ds(first - 1, 8), :] + qp[pl.ds(first + 1, 8), :]
        total = total + jnp.where(place < 2, pltpu.roll(here, 1, 1), pltpu.roll(here, 127, 1))
        total = total + jnp.where(lane < 4, 0.0, pltpu.roll(here, 4, 1))
        total = total + jnp.where(lane >= 60, 0.0, pltpu.roll(here, 124, 1))
        inverse = h_inv[rows, :]
        h_mid[rows, :] = beside(inverse * (qn[rows, :] + total))
        h_inv[rows, :] = beside(inverse)

    @pl.loop(0, groups)
    def _(b):
        rows = pl.ds(pl.multiple_of(8 + b * 8, 8), 8)
        h_init[rows, :] = beside(qp[rows, :])

    @pl.loop(0, br // 8)
    def _(b):
        fwd[0, pl.ds(pl.multiple_of(b * 8, 8), 8), :] = jnp.zeros((8, BC), F32)

    def sweep(step, do_initial, do_middle, do_smooth):
        pending = []
        low, high = (0, groups) if do_middle else (1, groups - 1)
        for g in range(low, high):
            pending.append(group(refs[:10], step, 8 + 8 * g, do_initial, do_middle, do_smooth and 1 <= g < groups - 1))
            if len(pending) > LAG:
                put(pending.pop(0))
        for stores in pending:
            put(stores)

    for step in range(2):
        wait_bytes(noise_x.at[step, TOP:end, :], bulk_recv.at[step])

        @pl.loop(0, groups)
        def _(b):
            put(group(refs[:10], step, pl.multiple_of(8 + b * 8, 8), True, step > 0, False))

    @pl.loop(2, NL - 1)
    def _(step):
        wait_bytes(noise_x.at[step, TOP:end, :], bulk_recv.at[step])
        sweep(step, True, True, True)

    wait_bytes(noise_x.at[NL - 1, TOP:end, :], bulk_recv.at[NL - 1])

    wait_bytes(noise.at[:, :, :(nd - 1) * BC], bulk_send)

    wait_bytes(q_send.at[:nd - 1], q_ssem)

    @pl.when((d == 0) | (d == nd - 1))
    def _():
        wait_bytes(rows_send, r_ssem)
        wait_bytes(q_send, qh_ssem)


def back_kernel(*refs):
    fwd, kap = refs[:2]
    out, solution_x, out_sem = refs[10:]
    size = WB // 8
    steps = fwd.shape[1] // WB

    def result(b):
        rows = pl.ds(b * WB, WB)
        return pltpu.make_async_copy(solution_x.at[:, rows, :], out.at[:, rows, :], out_sem.at[b])

    def sweep_group(step, g, do_initial, do_middle):
        inside = 0 < g < last
        if not 0 <= g <= last or not (inside or do_middle):
            return []
        return group(refs[:10], step, 8 + 8 * g, do_initial, do_middle, inside)

    def back(g):
        rows = pl.ds(8 * g - 8, 8)
        for c in COLS:
            solved = fwd[NL - 1, rows, c]
            solution_x[NL - 1, rows, c] = solved
            for layer in range(NL - 2, -1, -1):
                solved = fwd[layer, rows, c] + kap[layer, rows, c] * solved
                solution_x[layer, rows, c] = solved

    last = steps * size + 1
    pending = []
    for turn in range(last + 7):
        pending.append([])
        if len(pending) > 1:
            put(pending.pop(0))
        for lag, stage in ((0, (NL - 1, True, True)), (2, (NL, False, True)), (4, (NL + 1, False, False))):
            pending[-1] += sweep_group(stage[0], turn - lag, *stage[1:])
        g = turn - 6
        if 0 < g < last:
            back(g)
            if g % size == 0:
                result(g // size - 1).start()

    for b in range(steps):
        result(b).wait()


def body(noise, kappa, mask):
    na, nd = lax.axis_size("ax"), lax.axis_size("ay")
    br = nd * SR
    ext = br + 2 * TOP
    dma = pltpu.SemaphoreType.DMA
    scratch = [
        pltpu.VMEM((NL, SR, nd * BC), F32),
        pltpu.VMEM((br, BC), jnp.int32),
        pltpu.VMEM((NL // 4, 8, nd * BC), F32),
        pltpu.VMEM((2, NL // 4, 8, BC), F32),
        pltpu.VMEM((2, NL // 4, 8, BC), F32),
        pltpu.VMEM((2, NL // 4, 8, BC), F32),
        pltpu.VMEM((nd, 8, 128), F32),
        pltpu.VMEM((nd + 2, 8, 128), F32),
        pltpu.VMEM((ext, 128), F32),
        pltpu.VMEM((ext, 128), F32),
        pltpu.VMEM((br, 128), F32),
        pltpu.VMEM((2, br // 4, 128), F32),
        pltpu.VMEM((2, br // 4, 128), F32),
        pltpu.VMEM((2, 2, 8, 128), F32),
        dma((3,)), dma, dma((NL,)),
        dma, dma,
        dma, dma((2,)),
        dma, dma((2,)),
        dma((2,)), dma((2,)),
        dma((2,)), dma((2,)),
        dma((2, 2)), dma((2, 2)),
    ]
    field = pltpu.VMEM((NL, br, BC), F32)
    fields = (
        field, field,
        pltpu.VMEM((NL, ext, BC), F32),
        pltpu.VMEM((NL, ext, BC), F32),
        pltpu.VMEM((NL + 2, 2, ext, 128), F32),
        pltpu.VMEM((NL + 2, 2, ext, 128), F32),
        pltpu.VMEM((NL, ext, 128), F32),
        pltpu.VMEM((ext, 128), F32),
        pltpu.VMEM((ext, 128), F32),
        pltpu.VMEM((ext, 128), F32),
    )
    fields = pl.pallas_call(
        functools.partial(kernel, na, nd),
        out_shape=fields,
        in_specs=[pl.BlockSpec(memory_space=pltpu.HBM)] * 3,
        out_specs=[pl.BlockSpec(memory_space=pltpu.VMEM)] * 10,
        scratch_shapes=scratch,
        compiler_params=pltpu.CompilerParams(collective_id=0, has_side_effects=True, vmem_limit_bytes=16 << 20),
        name="sweeps",
    )(*(pltpu.with_memory_space_constraint(x, pltpu.HBM) for x in (noise, kappa, mask)))
    return pl.pallas_call(
        back_kernel,
        out_shape=jax.ShapeDtypeStruct((NL, br, BC), F32),
        in_specs=[pl.BlockSpec(memory_space=pltpu.VMEM)] * 10,
        out_specs=pl.BlockSpec(memory_space=pltpu.HBM),
        scratch_shapes=[field, dma((br // WB,))],
        compiler_params=pltpu.CompilerParams(vmem_limit_bytes=16 << 20),
        name="back",
    )(*fields)


def solution(mesh):
    in_specs = (P(None, ("ax", "ay"), None), P(None, "ax", "ay"), P("ax", "ay"))
    out_specs = P(None, "ax", "ay")
    return jax.shard_map(body, mesh=mesh, in_specs=in_specs, out_specs=out_specs, check_vma=False)
```

```python
import functools

import jax
import jax.numpy as jnp
from jax import lax
from jax.experimental import pallas as pl
from jax.experimental.pallas import tpu as pltpu
from jax.sharding import PartitionSpec as P

MESH = pl.DeviceIdType.MESH
F32 = jnp.float32
NL = 16
SR = 16
BC = 256
TOP = 16
LAG = 2
RB = 32
COLS = (slice(0, 128), slice(128, 256))
EARLY = 4


def wait_bytes(ref, sem):
    pltpu.make_async_copy(ref, ref, sem).wait()


def around(field, layer, first, here, outer):
    rows = pl.ds(first, 8)
    lane = lax.broadcasted_iota(jnp.int32, (8, 128), 1)
    lane_l, lane_r = lane == 0, lane == 127
    back = [pltpu.roll(x, 1, 1) for x in here]
    fore = [pltpu.roll(x, 127, 1) for x in here]
    side = (
        jnp.where(lane_l, outer, back[0]) + jnp.where(lane_r, fore[1], fore[0]),
        jnp.where(lane_l, back[0], back[1]) + jnp.where(lane_r, outer, fore[1]),
    )
    return [
        side[c] + (field[layer + 1, c, pl.ds(first - 1, 8), :] + field[layer + 1, c, pl.ds(first + 1, 8), :])
        + field[layer, c, rows, :]
        for c in range(2)
    ]

def group(refs, step, first, do_initial, do_middle, do_smooth):
    fwd, kap, noise_x, inv_x, init_x, mid_x, mid_h, h_init, h_mid, h_inv = refs
    rows = pl.ds(first, 8)
    lane = lax.broadcasted_iota(jnp.int32, (8, 128), 1)
    stores = []
    initial = middle = None
    if do_initial:
        initial = [inv_x[step, rows, COLS[c]] * noise_x[step, rows, COLS[c]] for c in range(2)]
        stores += [(init_x, (step + 1, c, rows, slice(None)), initial[c]) for c in range(2)]
    if do_middle:
        layer = step - 1
        turn = lax.rem(254 - 4 * layer, 128)
        here = [init_x[layer + 1, c, rows, :] for c in range(2)]
        total = around(init_x, layer, first, here, pltpu.roll(h_init[rows, :], turn, 1))
        if initial is not None:
            total = [total[c] + initial[c] for c in range(2)]
        middle = [inv_x[layer, rows, COLS[c]] * (noise_x[layer, rows, COLS[c]] + total[c]) for c in range(2)]
        inner = jnp.where(lane < 64, here[0], here[1])
        outer = pltpu.roll(h_mid[rows, :], turn, 1) + pltpu.roll(h_inv[rows, :], turn, 1) * inner
        stores += [(mid_x, (layer + 1, c, rows, slice(None)), middle[c]) for c in range(2)]
        stores += [(mid_h, (layer, rows, slice(None)), outer)]
    if do_smooth:
        layer = step - 2
        own = pl.ds(pl.multiple_of(first - TOP, 8), 8)
        here = [mid_x[layer + 1, c, rows, :] for c in range(2)]
        total = around(mid_x, layer, first, here, mid_h[layer, rows, :])
        if middle is not None:
            total = [total[c] + middle[c] for c in range(2)]
        for c in range(2):
            field = inv_x[layer, rows, COLS[c]] * (noise_x[layer, rows, COLS[c]] + total[c])
            previous = fwd[lax.max(layer - 1, 0), own, COLS[c]]
            pivot = kap[layer, own, COLS[c]]
            stores += [(fwd, (layer, own, COLS[c]), (field + previous) * pivot)]
    return stores


def put(stores):
    for ref, index, value in stores:
        ref[index] = value


def kernel(na, nd, noise, kappa, mask, *refs):
    fwd, kap, noise_x, inv_x, init_x, mid_x, mid_h, h_init, h_mid, h_inv = refs[:10]
    (strip, msk, rows_send, rowi_send, rown, rowi, q_send, q_recv, qn, qp, e_send, f_send, f_recv, c_recv, load_sem, bulk_send, bulk_recv, q_ssem, q_rsem, r_ssem, r_rsem, qh_ssem, qh_rsem,
     e_ssem, e_rsem, i_ssem, i_rsem, c_ssem, c_rsem) = refs[10:]
    br = nd * SR
    end = TOP + br
    a, d = lax.axis_index("ax"), lax.axis_index("ay")
    above, below = lax.rem(a + na - 1, na), lax.rem(a + 1, na)
    left, right = lax.rem(d + nd - 1, nd), lax.rem(d + 1, nd)

    loads = [
        pltpu.make_async_copy(noise, strip, load_sem.at[0]),
        pltpu.make_async_copy(kappa, kap, load_sem.at[1]),
        pltpu.make_async_copy(mask, msk, load_sem.at[2]),
    ]
    for load in loads:
        load.start()

    barrier = pltpu.get_barrier_semaphore()

    def greet(x, y):
        pl.semaphore_signal(barrier, inc=1, device_id=(x, y), device_id_type=MESH)

    for k in range(1, nd):
        greet(a, lax.rem(d + k, nd))

    edge = jnp.where(d == 0, nd, 0) + jnp.where(d == nd - 1, nd, 0)
    odd = lax.rem(a, 2)

    @pl.when(odd == 0)
    def _():
        for k in range(nd):
            greet(above, lax.rem(d + k, nd))
            greet(below, lax.rem(d + k, nd))

    pl.semaphore_wait(barrier, nd - 1 + odd * (2 * nd))

    @pl.when(odd == 1)
    def _():
        for x in (above, below):
            for y in (d, left, right):
                greet(x, y)
        greet(above, nd - 1)
        greet(below, 0)
        for y, x in ((0, above), (nd - 1, below)):
            @pl.when(d == y)
            def _():
                @pl.loop(0, nd)
                def _(t):
                    greet(x, t)

    def bulk(layer):
        pltpu.make_async_copy(
            noise.at[layer, :, pl.ds(pl.multiple_of(d * BC, BC), BC)],
            noise_x.at[layer, pl.ds(pl.multiple_of(TOP + d * SR, SR), SR), :],
            bulk_recv.at[layer],
        ).start()

        for k in range(1, nd):
            t = lax.rem(d + k, nd)
            pltpu.make_async_remote_copy(
                src_ref=noise.at[layer, :, pl.ds(pl.multiple_of(t * BC, BC), BC)],
                dst_ref=noise_x.at[layer, pl.ds(pl.multiple_of(TOP + d * SR, SR), SR), :],
                send_sem=bulk_send,
                recv_sem=bulk_recv.at[layer],
                device_id=(a, t),
                device_id_type=MESH,
            ).start()

    @pl.loop(0, EARLY)
    def _(layer):
        bulk(layer)

    lane = lax.broadcasted_iota(jnp.int32, (8, 128), 1)
    sub = lax.broadcasted_iota(jnp.int32, (8, BC), 0)

    loads[0].wait()

    @pl.loop(0, nd)
    def _(t):
        before = pl.multiple_of(lax.rem(t + nd - 1, nd) * BC + 128, 128)
        after = pl.multiple_of(lax.rem(t + 1, nd) * BC, 128)
        packed = jnp.zeros((8, 128), F32)
        for layer in range(NL):
            for half in range(2):
                rows = slice(half * 8, half * 8 + 8)
                both = jnp.where(lane < 64, strip[layer, rows, pl.ds(after, 128)], strip[layer, rows, pl.ds(before, 128)])
                packed = jnp.where(lane // 4 == layer + 16 * half, pltpu.roll(both, (4 * layer + 2 + 64 * half) % 128, 1), packed)
        q_send[t] = packed

    def q_place(s):
        return q_recv.at[s + 1]

    pltpu.make_async_copy(q_send.at[d], q_place(d), q_rsem).start()

    @pl.loop(1, nd)
    def _(k):
        t = lax.rem(d + k, nd)
        pltpu.make_async_remote_copy(
            src_ref=q_send.at[t], dst_ref=q_place(d), send_sem=q_ssem, recv_sem=q_rsem,
            device_id=(a, t), device_id_type=MESH,
        ).start()

    def pick_rows(tile, first, i):
        return pltpu.roll(tile, (2 * i - first) % 8, 0)

    def send_rows(first_row, first, x, slot):
        @pl.loop(0, nd)
        def _(t):
            cols = pl.ds(pl.multiple_of(t * BC, BC), BC)
            for q in range(NL // 4):
                packed = jnp.zeros((8, BC), F32)
                for i in range(4):
                    tile = strip[4 * q + i, first_row:first_row + 8, cols]
                    packed = jnp.where(sub // 2 == i, pick_rows(tile, first, i), packed)
                rows_send[q, :, cols] = packed
            pltpu.make_async_remote_copy(
                src_ref=rows_send.at[:, :, cols], dst_ref=rown.at[slot], send_sem=r_ssem, recv_sem=r_rsem.at[slot],
                device_id=(x, t), device_id_type=MESH,
            ).start()
            pltpu.make_async_remote_copy(
                src_ref=q_send.at[t], dst_ref=q_recv.at[(0, nd + 1)[slot]], send_sem=qh_ssem,
                recv_sem=qh_rsem.at[slot], device_id=(x, t), device_id_type=MESH,
            ).start()

    @pl.when(odd == 0)
    def _():
        pl.semaphore_wait(barrier, 8 + edge)

    @pl.when(d == 0)
    def _():
        send_rows(0, 0, above, 1)

    @pl.when(d == nd - 1)
    def _():
        send_rows(SR - 8, 6, below, 0)

    loads[1].wait()
    loads[2].wait()
    rb = 32
    lane_b = lax.broadcasted_iota(jnp.int32, (rb, 128), 1)

    @pl.loop(0, br // rb)
    def _(b):
        rows = pl.ds(pl.multiple_of(b * rb, rb), rb)
        active = msk[rows, :].astype(F32)
        packed = jnp.zeros((rb, 128), F32)
        for layer in range(NL):
            inverse = active / (6.0 + kap[layer, rows, :])
            inv_x[layer, pl.ds(pl.multiple_of(TOP + b * rb, 16), rb), :] = inverse
            both = jnp.where(lane_b < 64, inverse[:, :128], inverse[:, 128:])
            packed = jnp.where(lane_b // 4 == layer, pltpu.roll(both, (4 * layer + 2) % 128, 1), packed)
        e_send[rows, :] = packed

    folds = ((0, 2, 64, 66), (0, 126, 64, 62))
    fr = br // 4
    place = lane % 4

    @pl.loop(0, fr // 8)
    def _(b):
        for slot in range(2):
            packed = jnp.zeros((8, 128), F32)
            for k in range(4):
                piece = pltpu.roll(e_send[pl.ds(pl.multiple_of(k * fr + b * 8, 8), 8), :], folds[slot][k], 1)
                low = (0, 2, 0, 2)[k] if slot == 0 else (2, 0, 2, 0)[k]
                mine = (place >= low) & (place < low + 2) & (lane // 64 == k // 2)
                packed = jnp.where(mine, piece, packed)
            f_send[slot, pl.ds(pl.multiple_of(b * 8, 8), 8), :] = packed

    halos = []
    for slot, y in ((0, right), (1, left)):
        halos.append(pltpu.make_async_remote_copy(
            src_ref=f_send.at[slot], dst_ref=f_recv.at[slot], send_sem=e_ssem.at[slot], recv_sem=e_rsem.at[slot],
            device_id=(a, y), device_id_type=MESH,
        ))
        halos.append(pltpu.make_async_remote_copy(
            src_ref=e_send.at[br - 8:br, :], dst_ref=c_recv.at[slot, 0], send_sem=c_ssem.at[slot, 0],
            recv_sem=c_rsem.at[slot, 0], device_id=(below, y), device_id_type=MESH,
        ))
        halos.append(pltpu.make_async_remote_copy(
            src_ref=e_send.at[0:8, :], dst_ref=c_recv.at[slot, 1], send_sem=c_ssem.at[slot, 1],
            recv_sem=c_rsem.at[slot, 1], device_id=(above, y), device_id_type=MESH,
        ))
    for q in range(NL // 4):
        down = jnp.zeros((8, BC), F32)
        up = jnp.zeros((8, BC), F32)
        for i in range(4):
            layer = 4 * q + i
            down = jnp.where(sub // 2 == i, pick_rows(inv_x[layer, end - 8:end, :], 6, i), down)
            up = jnp.where(sub // 2 == i, pick_rows(inv_x[layer, TOP:TOP + 8, :], 0, i), up)
        rowi_send[0, q] = down
        rowi_send[1, q] = up
    for slot, x in ((0, below), (1, above)):
        halos.append(pltpu.make_async_remote_copy(
            src_ref=rowi_send.at[slot], dst_ref=rowi.at[slot], send_sem=i_ssem.at[slot], recv_sem=i_rsem.at[slot],
            device_id=(x, d), device_id_type=MESH,
        ))
    for halo in halos:
        halo.start()

    @pl.loop(EARLY, NL)
    def _(layer):
        bulk(layer)

    @pl.loop(0, br // rb)
    def _(b):
        rows = pl.ds(pl.multiple_of(b * rb, rb), rb)
        pivot = jnp.zeros((rb, BC), F32)
        for layer in range(NL):
            pivot = 1.0 / (2.5 + kap[layer, rows, :] - pivot)
            kap[layer, rows, :] = pivot

    @pl.loop(0, (br + 16) // 16)
    def _(b):
        rows = pl.ds(pl.multiple_of(8 + b * 16, 8), 16)
        for field in (init_x, mid_x):
            for layer in (0, NL + 1):
                for c in range(2):
                    field[layer, c, rows, :] = jnp.zeros((16, 128), F32)

    for halo in halos:
        halo.wait()
    for slot in range(2):
        wait_bytes(rown.at[slot], r_rsem.at[slot])
        wait_bytes(q_recv.at[slot], qh_rsem.at[slot])
    wait_bytes(q_recv.at[1:nd + 1], q_rsem)
    keep_top = jnp.where(a > 0, 1.0, 0.0).astype(F32)
    keep_end = jnp.where(a < na - 1, 1.0, 0.0).astype(F32)
    keep_left = jnp.where(d > 0, 1.0, 0.0).astype(F32)
    keep_right = jnp.where(d < nd - 1, 1.0, 0.0).astype(F32)

    @pl.loop(0, NL // 4)
    def _(q):
        for i in range(4):
            layer = 4 * q + i
            inv_x[layer, TOP - 8:TOP, :] = keep_top * pltpu.roll(rowi[0, q], (6 - 2 * i) % 8, 0)
            inv_x[layer, end:end + 8, :] = keep_end * pltpu.roll(rowi[1, q], (-2 * i) % 8, 0)
            noise_x[layer, TOP - 8:TOP, :] = pltpu.roll(rown[0, q], (6 - 2 * i) % 8, 0)
            noise_x[layer, end:end + 8, :] = pltpu.roll(rown[1, q], (-2 * i) % 8, 0)

    groups = (br + 16) // 8

    def beside(packed):
        return jnp.where(place == 1, pltpu.roll(packed, 127, 1), pltpu.roll(packed, 1, 1))

    def sides(first, from_left, from_right, noise_q):
        rows = pl.ds(first, 8)
        inverse = jnp.where(place < 2, from_left * keep_left, from_right * keep_right)
        qn[rows, :] = noise_q
        qp[rows, :] = inverse * noise_q
        h_inv[rows, :] = inverse

    sides(TOP - 8, c_recv[0, 0] * keep_top, c_recv[1, 0] * keep_top, pltpu.roll(q_recv[0], 64, 1))
    sides(end, c_recv[0, 1] * keep_end, c_recv[1, 1] * keep_end, q_recv[nd + 1])
    for k in range(4):
        @pl.loop(0, fr // SR)
        def _(b):
            noise_q = q_recv[1 + k * (fr // SR) + b]
            for half in range(2):
                rows = pl.ds(pl.multiple_of(b * SR + half * 8, 8), 8)
                pieces = [pltpu.roll(f_recv[slot, rows, :], (128 - folds[slot][k]) % 128, 1) for slot in range(2)]
                first = pl.multiple_of(TOP + k * fr + b * SR + half * 8, 8)
                sides(first, *pieces, pltpu.roll(noise_q, 64, 1) if half else noise_q)

    @pl.loop(0, br // 8)
    def _(b):
        first = pl.multiple_of(TOP + b * 8, 8)
        rows = pl.ds(first, 8)
        here = qp[rows, :]
        total = qp[pl.ds(first - 1, 8), :] + qp[pl.ds(first + 1, 8), :]
        total = total + jnp.where(place < 2, pltpu.roll(here, 1, 1), pltpu.roll(here, 127, 1))
        total = total + jnp.where(lane < 4, 0.0, pltpu.roll(here, 4, 1))
        total = total + jnp.where(lane >= 60, 0.0, pltpu.roll(here, 124, 1))
        inverse = h_inv[rows, :]
        h_mid[rows, :] = beside(inverse * (qn[rows, :] + total))
        h_inv[rows, :] = beside(inverse)

    @pl.loop(0, groups)
    def _(b):
        rows = pl.ds(pl.multiple_of(8 + b * 8, 8), 8)
        h_init[rows, :] = beside(qp[rows, :])

    @pl.loop(0, br // 8)
    def _(b):
        fwd[0, pl.ds(pl.multiple_of(b * 8, 8), 8), :] = jnp.zeros((8, BC), F32)

    def sweep(step, do_initial, do_middle, do_smooth):
        pending = []
        low, high = (0, groups) if do_middle else (1, groups - 1)
        for g in range(low, high):
            pending.append(group(refs[:10], step, 8 + 8 * g, do_initial, do_middle, do_smooth and 1 <= g < groups - 1))
            if len(pending) > LAG:
                put(pending.pop(0))
        for stores in pending:
            put(stores)

    for step in range(2):
        wait_bytes(noise_x.at[step, TOP:end, :], bulk_recv.at[step])

        @pl.loop(0, groups)
        def _(b):
            put(group(refs[:10], step, pl.multiple_of(8 + b * 8, 8), True, step > 0, False))

    @pl.loop(2, NL - 1)
    def _(step):
        wait_bytes(noise_x.at[step, TOP:end, :], bulk_recv.at[step])
        sweep(step, True, True, True)

    wait_bytes(noise_x.at[NL - 1, TOP:end, :], bulk_recv.at[NL - 1])

    wait_bytes(noise.at[:, :, :(nd - 1) * BC], bulk_send)

    wait_bytes(q_send.at[:nd - 1], q_ssem)

    @pl.when((d == 0) | (d == nd - 1))
    def _():
        wait_bytes(rows_send, r_ssem)
        wait_bytes(q_send, qh_ssem)


def back_kernel(*refs):
    fwd, kap = refs[:2]
    out, solution_x, out_sem = refs[10:]
    size = RB // 8
    steps = fwd.shape[1] // RB

    def result(b):
        rows = pl.ds(b * RB, RB)
        return pltpu.make_async_copy(solution_x.at[:, rows, :], out.at[:, rows, :], out_sem.at[b])

    def sweep_group(step, g, do_initial, do_middle):
        inside = 0 < g < last
        if not 0 <= g <= last or not (inside or do_middle):
            return []
        return group(refs[:10], step, 8 + 8 * g, do_initial, do_middle, inside)

    def back(g):
        rows = pl.ds(8 * g - 8, 8)
        for c in COLS:
            solved = fwd[NL - 1, rows, c]
            solution_x[NL - 1, rows, c] = solved
            for layer in range(NL - 2, -1, -1):
                solved = fwd[layer, rows, c] + kap[layer, rows, c] * solved
                solution_x[layer, rows, c] = solved

    last = steps * size + 1
    pending = []
    for turn in range(last + 10):
        pending.append([])
        if len(pending) > LAG:
            put(pending.pop(0))
        for lag, stage in ((0, (NL - 1, True, True)), (3, (NL, False, True)), (6, (NL + 1, False, False))):
            pending[-1] += sweep_group(stage[0], turn - lag, *stage[1:])
        g = turn - 9
        if 0 < g < last:
            back(g)
            if g % size == 0:
                result(g // size - 1).start()

    for b in range(steps):
        result(b).wait()


def body(noise, kappa, mask):
    na, nd = lax.axis_size("ax"), lax.axis_size("ay")
    br = nd * SR
    ext = br + 2 * TOP
    dma = pltpu.SemaphoreType.DMA
    scratch = [
        pltpu.VMEM((NL, SR, nd * BC), F32),
        pltpu.VMEM((br, BC), jnp.int32),
        pltpu.VMEM((NL // 4, 8, nd * BC), F32),
        pltpu.VMEM((2, NL // 4, 8, BC), F32),
        pltpu.VMEM((2, NL // 4, 8, BC), F32),
        pltpu.VMEM((2, NL // 4, 8, BC), F32),
        pltpu.VMEM((nd, 8, 128), F32),
        pltpu.VMEM((nd + 2, 8, 128), F32),
        pltpu.VMEM((ext, 128), F32),
        pltpu.VMEM((ext, 128), F32),
        pltpu.VMEM((br, 128), F32),
        pltpu.VMEM((2, br // 4, 128), F32),
        pltpu.VMEM((2, br // 4, 128), F32),
        pltpu.VMEM((2, 2, 8, 128), F32),
        dma((3,)), dma, dma((NL,)),
        dma, dma,
        dma, dma((2,)),
        dma, dma((2,)),
        dma((2,)), dma((2,)),
        dma((2,)), dma((2,)),
        dma((2, 2)), dma((2, 2)),
    ]
    field = pltpu.VMEM((NL, br, BC), F32)
    fields = (
        field, field,
        pltpu.VMEM((NL, ext, BC), F32),
        pltpu.VMEM((NL, ext, BC), F32),
        pltpu.VMEM((NL + 2, 2, ext, 128), F32),
        pltpu.VMEM((NL + 2, 2, ext, 128), F32),
        pltpu.VMEM((NL, ext, 128), F32),
        pltpu.VMEM((ext, 128), F32),
        pltpu.VMEM((ext, 128), F32),
        pltpu.VMEM((ext, 128), F32),
    )
    fields = pl.pallas_call(
        functools.partial(kernel, na, nd),
        out_shape=fields,
        in_specs=[pl.BlockSpec(memory_space=pltpu.HBM)] * 3,
        out_specs=[pl.BlockSpec(memory_space=pltpu.VMEM)] * 10,
        scratch_shapes=scratch,
        compiler_params=pltpu.CompilerParams(collective_id=0, has_side_effects=True, vmem_limit_bytes=16 << 20),
        name="sweeps",
    )(*(pltpu.with_memory_space_constraint(x, pltpu.HBM) for x in (noise, kappa, mask)))
    return pl.pallas_call(
        back_kernel,
        out_shape=jax.ShapeDtypeStruct((NL, br, BC), F32),
        in_specs=[pl.BlockSpec(memory_space=pltpu.VMEM)] * 10,
        out_specs=pl.BlockSpec(memory_space=pltpu.HBM),
        scratch_shapes=[field, dma((br // RB,))],
        compiler_params=pltpu.CompilerParams(vmem_limit_bytes=16 << 20),
        name="back",
    )(*fields)


def solution(mesh):
    in_specs = (P(None, ("ax", "ay"), None), P(None, "ax", "ay"), P("ax", "ay"))
    out_specs = P(None, "ax", "ay")
    return jax.shard_map(body, mesh=mesh, in_specs=in_specs, out_specs=out_specs, check_vma=False)
```
